32 devices in a mesh: freq: 4 (over x, core), frame: 8 (over z, y).
Axes of the slice: x: 2, y: 2, z: 4, core: 2. Of those that a mesh axis runs over, the one named last changes fastest.
Arguments:
- spectra: bfloat16 [2, 24, 1024, 2048], P(None, None, 'freq', 'frame'), may hold values from -6 to 6
- norm_gain: float32 [1024], replicated, may hold values from 0.25 to 1.75
- w_in: bfloat16 [1024, 1024], replicated, may hold values from -0.1875 to 0.1875
- b_in: float32 [1024], replicated, may hold values from -3 to 3
- w_mid: bfloat16 [1024, 1024], replicated, may hold values from -0.1875 to 0.1875
- b_mid: float32 [1024], replicated, may hold values from -3 to 3
- w_out: bfloat16 [1024, 1024], replicated, may hold values from -0.1875 to 0.1875
- b_out: float32 [1024], replicated, may hold values from -3 to 3
Outputs:
- demixed: float32 [2, 24, 1024, 2048], P(None, None, 'freq', 'frame')
- variances: bfloat16 [24, 1024, 2048], P(None, 'freq', 'frame')
The draws below stay inside these ranges and needn't reach their ends.
All inputs are finite; a program needn't handle non-finite values.
Results may differ from the reference program's by a relative error of at most 0.0032.
Values may be sent and summed in bfloat16 or wider, within the bound.
No kernel may reach another device: no remote copies, remote signals or barrier semaphores. Data moves between devices by JAX's collectives and lax.ppermute only.
A program may use at most 128 MiB of HBM per device.

```python
import jax
import jax.numpy as jnp
from jax import lax

K = 24
F = 1024
H = 1024
FRAMES = 2048


def draw_spectra(key, part):
    keys = jax.random.split(jax.random.fold_in(key, 7301), 5)
    shape = (2, K, F, FRAMES)
    independent = jax.random.normal(keys[0], shape, jnp.float32)
    shared = jax.random.normal(keys[1], (2, 1, F, FRAMES), jnp.float32)
    loading = jax.random.uniform(keys[2], (1, K, 1, 1), jnp.float32, 0.7, 1.3)
    source_scale = jnp.exp(jax.random.uniform(keys[3], (1, K, 1, 1), jnp.float32, -0.5, 0.47))
    slope = jax.random.uniform(keys[4], (FRAMES,), jnp.float32, -1.0, 1.0)
    position = 2.0 * jnp.arange(F, dtype=jnp.float32) / F - 1.0
    tilt = jnp.exp(0.8 * slope[None, :] * position[:, None])
    values = (independent + loading * shared) * tilt[None, None, :, :] * source_scale
    return jnp.clip(values, -6.0, 6.0).astype(jnp.bfloat16)


def noise(stream_key, dims, scale, limit, held_as=jnp.bfloat16):
    result = scale * jax.random.normal(stream_key, dims, jnp.float32)
    return jnp.clip(result, min=-limit, max=limit).astype(held_as)


def setup_inputs(seed: int = 0) -> dict:
    splits = jax.random.split(jax.random.key(seed), 9)
    spectra = draw_spectra(jax.random.fold_in(splits[8], 71), 0)
    norm_gain = jnp.clip(1.0 + 0.15 * jax.random.normal(splits[1], (F,), jnp.float32), 0.25, 1.75)
    w_in = noise(splits[2], (F, H), F ** -0.5, 0.1875)
    b_in = noise(splits[3], (H,), 0.5, 3.0, jnp.float32)
    w_mid = noise(splits[4], (H, H), H ** -0.5, 0.1875)
    b_mid = noise(splits[5], (H,), 0.5, 3.0, jnp.float32)
    w_out = noise(splits[6], (H, F), H ** -0.5, 0.1875)
    b_out = noise(splits[7], (F,), 0.5, 3.0, jnp.float32)
    return {"spectra": spectra, "norm_gain": norm_gain, "w_in": w_in, "b_in": b_in, "w_mid": w_mid, "b_mid": b_mid, "w_out": w_out, "b_out": b_out}


epsilon = 1e-05
power_floor = 0.001
variance_floor = 0.25

def source_model(logpower, norm_gain, w_in, b_in, w_mid, b_mid, w_out, b_out):
    values = logpower.astype(jnp.float32)
    average = lax.optimization_barrier(jnp.mean(values, axis=1, keepdims=True))
    centred = values - average
    spread = lax.optimization_barrier(jnp.mean(centred * centred, axis=1, keepdims=True))
    normed = (centred * lax.rsqrt(spread + epsilon) * norm_gain).astype(jnp.bfloat16)
    hidden_one = jax.nn.silu(jnp.dot(normed, w_in, preferred_element_type=jnp.float32) + b_in).astype(jnp.bfloat16)
    hidden_two = jax.nn.silu(jnp.dot(hidden_one, w_mid, preferred_element_type=jnp.float32) + b_mid).astype(jnp.bfloat16)
    output_pre = jnp.dot(hidden_two, w_out, preferred_element_type=jnp.float32) + b_out
    return (jax.nn.softplus(output_pre) + variance_floor).astype(jnp.bfloat16)

def reference(spectra, norm_gain, w_in, b_in, w_mid, b_mid, w_out, b_out):
    real_part = spectra[0].astype(jnp.float32)
    imag_part = spectra[1].astype(jnp.float32)
    logpower = jnp.log(real_part * real_part + imag_part * imag_part + power_floor).astype(jnp.bfloat16)

    def per_source(sheet):
        return source_model(sheet.T, norm_gain, w_in, b_in, w_mid, b_mid, w_out, b_out).T
    variances = lax.map(per_source, logpower)
    weight = 1.0 / variances.astype(jnp.float32)
    frames = spectra.shape[3]
    count = spectra.shape[1]

    def sweep(source, carry):
        demix_real, demix_imag = carry
        pick_real = lax.dynamic_index_in_dim(demix_real, source, 0, keepdims=False)
        pick_imag = lax.dynamic_index_in_dim(demix_imag, source, 0, keepdims=False)
        numer_real = lax.optimization_barrier(jnp.sum(weight * (demix_real * pick_real + demix_imag * pick_imag), axis=2)) / frames
        numer_imag = lax.optimization_barrier(jnp.sum(weight * (demix_imag * pick_real - demix_real * pick_imag), axis=2)) / frames
        denom = lax.optimization_barrier(jnp.sum(weight * (pick_real * pick_real + pick_imag * pick_imag), axis=2)) / frames
        is_self = (jnp.arange(count, dtype=jnp.int32) == source)[:, None]
        coef_real = jnp.where(is_self, 1.0 - lax.rsqrt(denom), numer_real / denom)[:, :, None]
        coef_imag = jnp.where(is_self, 0.0, numer_imag / denom)[:, :, None]
        new_real = demix_real - (coef_real * pick_real - coef_imag * pick_imag)
        new_imag = demix_imag - (coef_real * pick_imag + coef_imag * pick_real)
        return (new_real, new_imag)
    demix_real, demix_imag = lax.fori_loop(0, count, sweep, (real_part, imag_part))
    return (jnp.stack([demix_real, demix_imag]), variances)
```

```python
import functools

import jax
import jax.numpy as jnp
from jax import lax
from jax.experimental import pallas as pl
from jax.experimental.pallas import tpu as pltpu
from jax.sharding import PartitionSpec as P

epsilon = 1e-05
power_floor = 0.001
variance_floor = 0.25
GROUP = 8
LANES = 128
BF16 = jnp.bfloat16
F32 = jnp.float32
SMEM = pltpu.SMEM
VMEM = pltpu.VMEM


def options(mib=48):
    return pltpu.CompilerParams(vmem_limit_bytes=mib * 1024 * 1024)


def cost(flops, moved, transcendentals=0):
    return pl.CostEstimate(
        flops=int(flops), bytes_accessed=int(moved), transcendentals=int(transcendentals)
    )


def exchange(value, axis, mask):
    size = lax.axis_size(axis)
    return lax.ppermute(value, axis, [(i, i ^ mask) for i in range(size)])


def prepare_kernel(place, x_ref, *refs, owners, each, chunks, count):
    powers, l_ref, rows = refs[:-2], refs[-2], refs[-1]
    mine = place[0]
    bins, frames = x_ref.shape[2], x_ref.shape[3]
    for c in range(chunks):
        for m in range(owners):
            for i in range(each):
                source = c * GROUP + (mine ^ m) * each + i
                re = x_ref[0, source].astype(F32)
                im = x_ref[1, source].astype(F32)
                powers[c * owners + m][i] = jnp.log(re * re + im * im + power_floor).astype(BF16)
    wide = frames // LANES
    for i in range(wide):
        block = x_ref[:, :, :, i * LANES : (i + 1) * LANES].astype(F32)
        rows[i] = block.reshape(2 * count * bins, LANES)

    def one(f, carry):
        both = jnp.concatenate(
            [rows[i, pl.ds(f, 2 * count, stride=bins), :] for i in range(wide)], axis=1
        )
        re, im = both[:count], both[count:]
        upper = jnp.concatenate([re, im], axis=1)
        lower = jnp.concatenate([im, -re], axis=1)
        l_ref[f] = jnp.concatenate([upper, lower], axis=0).astype(BF16)
        return carry

    lax.fori_loop(0, bins, one, 0)


def prepare(spectra, place, owners, each, chunks):
    _, count, bins, frames = spectra.shape
    step = 16
    power = jax.ShapeDtypeStruct((each, bins, frames), BF16)
    shapes = [power] * (chunks * owners)
    shapes.append(jax.ShapeDtypeStruct((bins, 2 * count, 2 * frames), BF16))
    specs = [pl.BlockSpec((each, step, frames), lambda b: (0, b, 0))] * (chunks * owners)
    specs.append(pl.BlockSpec((step, 2 * count, 2 * frames), lambda b: (b, 0, 0)))
    return pl.pallas_call(
        functools.partial(
            prepare_kernel, owners=owners, each=each, chunks=chunks, count=count
        ),
        grid=(bins // step,),
        in_specs=[
            pl.BlockSpec(memory_space=SMEM),
            pl.BlockSpec((2, count, step, frames), lambda b: (0, 0, b, 0)),
        ],
        out_specs=specs,
        out_shape=shapes,
        scratch_shapes=[VMEM((frames // LANES, 2 * count * step, LANES), F32)],
        compiler_params=options(),
        cost_estimate=cost(20 * spectra.size, 8 * spectra.size, spectra.size // 2),
        name="prepare",
    )(place, spectra)


def silu(v):
    return v / (1.0 + jnp.exp(-v))


def softplus(v):
    return jnp.maximum(v, 0.0) + jnp.log1p(jnp.exp(-jnp.abs(v)))


def model_kernel(place, *refs, owners):
    pieces = refs[:owners]
    gain, w_in, b_in, w_mid, b_mid, w_out, b_out = refs[owners : owners + 7]
    outs = refs[owners + 7 : 2 * owners + 7]
    normed, hidden = refs[2 * owners + 7 :]
    mine = place[0]
    bins, frames = pieces[0].shape[1:]
    total = bins * owners
    wide = frames // LANES

    def spread(column):
        return jnp.concatenate([column] * wide, axis=1)

    values = [piece[0].astype(F32) for piece in pieces]
    average = sum(jnp.sum(v, axis=0, keepdims=True) for v in values) / total
    values = [v - average for v in values]
    square = sum(jnp.sum(v * v, axis=0, keepdims=True) for v in values) / total
    scale = lax.rsqrt(square + epsilon)
    for m in range(owners):
        at = pl.multiple_of((mine ^ m) * bins, bins)
        normed[pl.ds(at, bins), :] = (
            values[m] * scale * spread(gain[pl.ds(at, bins), :])
        ).astype(BF16)

    tile = 256

    def layer(weights, bias, source, target):
        def one(h, carry):
            at = pl.multiple_of(h * tile, tile)
            v = jnp.dot(weights[pl.ds(at, tile), :], source[...], preferred_element_type=F32)
            target[pl.ds(at, tile), :] = silu(v + spread(bias[pl.ds(at, tile), :])).astype(BF16)
            return carry

        lax.fori_loop(0, weights.shape[0] // tile, one, 0)

    layer(w_in, b_in, normed, hidden)
    layer(w_mid, b_mid, hidden, normed)
    for m in range(owners):
        at = pl.multiple_of((mine ^ m) * bins, bins)
        v = jnp.dot(w_out[pl.ds(at, bins), :], normed[...], preferred_element_type=F32)
        outs[m][0] = (softplus(v + spread(b_out[pl.ds(at, bins), :])) + variance_floor).astype(
            BF16
        )


def model(pieces, place, weights):
    owners = len(pieces)
    each, bins, frames = pieces[0].shape
    hidden = weights[1].shape[0]
    block = pl.BlockSpec((1, bins, frames), lambda i: (i, 0, 0))
    whole = [pl.BlockSpec(w.shape, lambda i: (0, 0)) for w in weights]
    return pl.pallas_call(
        functools.partial(model_kernel, owners=owners),
        grid=(each,),
        in_specs=[pl.BlockSpec(memory_space=SMEM)] + [block] * owners + whole,
        out_specs=[block] * owners,
        out_shape=[jax.ShapeDtypeStruct((each, bins, frames), BF16)] * owners,
        scratch_shapes=[VMEM((hidden, frames), BF16), VMEM((hidden, frames), BF16)],
        compiler_params=options(),
        cost_estimate=cost(
            6 * each * hidden * hidden * frames, 6 * hidden * hidden, 8 * each * hidden * frames
        ),
        name="source_model",
    )(place, *pieces, *weights)


def covariance_kernel(table, place, l_ref, *refs, owners, count):
    pieces, o_ref, weight = refs[:owners], refs[owners], refs[owners + 1]
    mine = place[0]
    each, bins, frames = pieces[0].shape
    for m in range(owners):
        for i in range(each):
            weight[(mine ^ m) * each + i] = 1.0 / pieces[m][i].astype(F32)
    shape = (count, GROUP * count)
    row = lax.broadcasted_iota(jnp.int32, shape, 0)
    column = lax.rem(lax.broadcasted_iota(jnp.int32, shape, 1), count)
    real = row <= column

    def packed(f):
        left = l_ref[f]
        top = left.astype(F32)[:count]
        parts = []
        for j in range(GROUP):
            w = weight[j, pl.ds(f, 1), :]
            parts.append(top * jnp.concatenate([w, w], axis=1))
        right = jnp.concatenate(parts, axis=0)
        high = right.astype(BF16)
        low = (right - high.astype(F32)).astype(BF16)
        dims = (((1,), (1,)), ((), ()))
        v = lax.dot_general(left, high, dims, preferred_element_type=F32)
        v = v + lax.dot_general(left, low, dims, preferred_element_type=F32)
        return jnp.where(real, v[:count], v[count:])

    def one(p, carry):
        o_ref[0, p] = jnp.concatenate([packed(p), packed(p + bins // 2)], axis=1)
        return carry

    lax.fori_loop(0, bins // 2, one, 0)


def covariance(table, place, stacked, pieces, count):
    owners, shares = len(pieces), table.shape[0]
    each, bins, frames = pieces[0].shape
    share = stacked.shape[0] // lax.axis_size("frame")
    piece = pl.BlockSpec((each, share, frames), lambda r, table, place: (0, table[r], 0))
    lanes = 2 * GROUP * count
    return pl.pallas_call(
        functools.partial(covariance_kernel, owners=owners, count=count),
        grid_spec=pltpu.PrefetchScalarGridSpec(
            num_scalar_prefetch=2,
            grid=(shares,),
            in_specs=[
                pl.BlockSpec(
                    (share,) + stacked.shape[1:], lambda r, table, place: (table[r], 0, 0)
                )
            ]
            + [piece] * owners,
            out_specs=pl.BlockSpec(
                (1, share // 2, count, lanes), lambda r, table, place: (r, 0, 0, 0)
            ),
            scratch_shapes=[VMEM((GROUP, share, frames), F32)],
        ),
        out_shape=jax.ShapeDtypeStruct((shares, share // 2, count, lanes), F32),
        compiler_params=options(),
        cost_estimate=cost(
            shares * share * 8 * count * count * GROUP * frames * 2,
            shares * share * (8 * count * frames + 4 * count * count * GROUP),
        ),
        name="covariance",
    )(table, place, stacked, *pieces)


def unpack_kernel(*refs, count, share, lanes_b):
    parts, o_ref, turned = refs[:-2], refs[-2], refs[-1]
    half = GROUP * count
    blocks = o_ref.shape[1]

    def turn(a, carry):
        v = parts[0][:, a, :]
        for part in parts[1:]:
            v = v + part[:, a, :]
        v = jnp.concatenate([v[:, :half], v[:, half:]], axis=0)
        turned[a, :, 0:share] = v.T
        return carry

    lax.fori_loop(0, count, turn, 0)

    def lay(a, carry):
        for g in range(blocks):
            re, im = [], []
            for i in range(lanes_b):
                b = g * lanes_b + i
                if b >= count:
                    re.append(jnp.zeros((GROUP, share), F32))
                    im.append(jnp.zeros((GROUP, share), F32))
                    continue
                low, high = jnp.minimum(a, b), jnp.maximum(a, b)
                sign = jnp.where(a > b, 1.0, jnp.where(a < b, -1.0, 0.0))
                re.append(turned[low, pl.ds(high, GROUP, stride=count), :][:, :share])
                im.append(turned[high, pl.ds(low, GROUP, stride=count), :][:, :share] * sign)
            o_ref[a, g, 0] = jnp.concatenate(re, axis=1)
            o_ref[a, g, 1] = jnp.concatenate(im, axis=1)
        return carry

    lax.fori_loop(0, count, lay, 0)


def unpack(parts, count, share):
    lanes_b = LANES // share
    blocks = -(-count // lanes_b)
    shape = (count, blocks, 2, GROUP, LANES)
    return pl.pallas_call(
        functools.partial(unpack_kernel, count=count, share=share, lanes_b=lanes_b),
        out_shape=jax.ShapeDtypeStruct(shape, F32),
        scratch_shapes=[VMEM((count, GROUP * count, LANES), F32)],
        compiler_params=options(),
        cost_estimate=cost(10 * parts[0].size, 4 * parts[0].size * (len(parts) + 2)),
        name="unpack",
    )(*parts)


def sweep_kernel(*refs, count, share, frames):
    chunks = count // GROUP
    v_refs, o_ref, wr, wi, diagonal, flat = refs[:chunks], *refs[chunks:]
    lanes_b = LANES // share
    blocks = v_refs[0].shape[1]
    full = (GROUP, LANES)
    sub = lax.broadcasted_iota(jnp.int32, full, 0)
    lane = lax.broadcasted_iota(jnp.int32, full, 1)
    group = [(lane >= i * share) & (lane < (i + 1) * share) for i in range(lanes_b)]
    zero = jnp.zeros(full, F32)

    def start(a, carry):
        for c in range(chunks):
            wr[a, c] = jnp.where(sub + c * GROUP == a, 1.0, 0.0)
            wi[a, c] = zero
        return carry

    lax.fori_loop(0, count, start, 0)
    for c in range(chunks):
        for g in range(blocks):
            for part in range(2):
                d = zero
                for s in range(GROUP):
                    d = jnp.where(sub == s, v_refs[c][c * GROUP + s, g, part], d)
                diagonal[c, g, part] = d

    def total(x):
        shift = share
        while shift < LANES:
            x = x + pltpu.roll(x, shift, 1)
            shift *= 2
        return x

    for k in range(count):
        ck, sk = divmod(k, GROUP)
        used = k // lanes_b + 1
        pick_r, pick_i = [], []
        for g in range(used):
            pr, pi = zero, zero
            for i in range(lanes_b):
                b = g * lanes_b + i
                if b <= k:
                    pr = jnp.where(group[i], wr[b, ck, sk : sk + 1, :], pr)
                    pi = jnp.where(group[i], wi[b, ck, sk : sk + 1, :], pi)
            pick_r.append(pr)
            pick_i.append(pi)

        def product(load):
            ur, ui = zero, zero
            for g in range(used):
                vr, vi = load(g, 0), load(g, 1)
                ur = ur + vr * pick_r[g] + vi * pick_i[g]
                ui = ui + vi * pick_r[g] - vr * pick_i[g]
            return ur, ui

        def gather(a, carry):
            out = []
            kr = wr[a, ck, sk : sk + 1, :]
            ki = wi[a, ck, sk : sk + 1, :]
            for c in range(chunks):
                nr, ni, de = carry[3 * c : 3 * c + 3]
                ur, ui = product(lambda g, part: v_refs[c][a, g, part])
                ar, ai = wr[a, c], wi[a, c]
                out.append(nr + ar * ur - ai * ui)
                out.append(ni + ar * ui + ai * ur)
                out.append(de + kr * ur - ki * ui)
            return tuple(out)

        sums = lax.fori_loop(0, k + 1, gather, (zero,) * (3 * chunks))
        steer = []
        for c in range(chunks):
            nr, ni, de = sums[3 * c : 3 * c + 3]
            if (c + 1) * GROUP > k + 1:
                ur, ui = product(lambda g, part: diagonal[c, g, part])
                later = sub + c * GROUP > k
                nr = nr + jnp.where(later, ur, 0.0)
                ni = ni + jnp.where(later, ui, 0.0)
            nr, ni, de = total(nr), total(ni), total(de)
            inverse = 1.0 / de
            vr, vi = nr * inverse, ni * inverse
            if c == ck:
                vr = jnp.where(sub == sk, 1.0 - lax.rsqrt(de / frames), vr)
                vi = jnp.where(sub == sk, 0.0, vi)
            steer.append((vr, vi))

        def update(a, carry):
            kr = jnp.broadcast_to(wr[a, ck, sk : sk + 1, :], full)
            ki = jnp.broadcast_to(wi[a, ck, sk : sk + 1, :], full)
            for c in range(chunks):
                vr, vi = steer[c]
                wr[a, c] = wr[a, c] - (vr * kr - vi * ki)
                wi[a, c] = wi[a, c] - (vr * ki + vi * kr)
            return carry

        lax.fori_loop(0, k + 1, update, 0)

    def pack(a, carry):
        for c in range(chunks):
            at = c * GROUP * 2 * count + a
            flat[pl.ds(at, GROUP, stride=2 * count), :] = wr[a, c]
            flat[pl.ds(at + count, GROUP, stride=2 * count), :] = -wi[a, c]
        return carry

    lax.fori_loop(0, count, pack, 0)
    for i in range(flat.shape[0] // LANES):
        o_ref[:, i * LANES : (i + 1) * LANES] = flat[i * LANES : (i + 1) * LANES, :].T[:share]


def sweep(parts, count, share, frames):
    chunks = count // GROUP
    blocks = parts[0].shape[1]
    state = VMEM((count, chunks, GROUP, LANES), F32)
    return pl.pallas_call(
        functools.partial(sweep_kernel, count=count, share=share, frames=frames),
        out_shape=jax.ShapeDtypeStruct((share, 2 * count * count), F32),
        scratch_shapes=[
            state,
            state,
            VMEM((chunks, blocks, 2, GROUP, LANES), F32),
            VMEM((2 * count * count, LANES), F32),
        ],
        compiler_params=options(),
        cost_estimate=cost(4500 * count**3, 4 * 3 * parts[0].size),
        name="sweep",
    )(*parts)


def apply_kernel(table, w_ref, l_ref, o_ref, mixing, rows, *, count):
    share = w_ref.shape[1]
    frames = o_ref.shape[3]
    wide = 2 * count
    tiles = frames // LANES
    pad = jnp.zeros((share, LANES - wide), F32)
    for j in range(count):
        v = jnp.concatenate([w_ref[0, :, j * wide : (j + 1) * wide], pad], axis=1)
        mixing[pl.ds(j, share, stride=count), :] = v

    def one(f, carry):
        at = pl.multiple_of(f * count, count)
        w = mixing[pl.ds(at, count), 0:wide]
        high = w.astype(BF16).astype(F32)
        middle = (w - high).astype(BF16).astype(F32)
        low = w - high - middle
        left = jnp.concatenate([high, middle, low], axis=0).astype(BF16)
        y = jnp.dot(left, l_ref[f], preferred_element_type=F32)
        y = y[:count] + (y[count : 2 * count] + y[2 * count :])
        for c in range(2):
            for i in range(tiles):
                v = y[:, c * frames + i * LANES : c * frames + (i + 1) * LANES]
                rows[i, pl.ds(c * count * share + f, count, stride=share), :] = v
        return carry

    lax.fori_loop(0, share, one, 0)
    for i in range(tiles):
        o_ref[:, :, :, i * LANES : (i + 1) * LANES] = rows[i].reshape(2, count, share, LANES)


def apply(table, mixing, stacked, count):
    shares, share = mixing.shape[:2]
    bins, frames = stacked.shape[0], stacked.shape[2] // 2
    return pl.pallas_call(
        functools.partial(apply_kernel, count=count),
        grid_spec=pltpu.PrefetchScalarGridSpec(
            num_scalar_prefetch=1,
            grid=(shares,),
            in_specs=[
                pl.BlockSpec((1,) + mixing.shape[1:], lambda r, table: (r, 0, 0)),
                pl.BlockSpec((share,) + stacked.shape[1:], lambda r, table: (table[r], 0, 0)),
            ],
            out_specs=pl.BlockSpec(
                (2, count, share, frames), lambda r, table: (0, 0, table[r], 0)
            ),
            scratch_shapes=[
                VMEM((share * count, LANES), F32),
                VMEM((frames // LANES, 2 * count * share, LANES), F32),
            ],
        ),
        out_shape=jax.ShapeDtypeStruct((2, count, bins, frames), F32),
        compiler_params=options(),
        cost_estimate=cost(
            16 * count * count * bins * frames, stacked.size * 2 + 8 * count * bins * frames
        ),
        name="apply",
    )(table, mixing, stacked)


def on_device(spectra, norm_gain, w_in, b_in, w_mid, b_mid, w_out, b_out):
    _, count, bins, frames = spectra.shape
    owners, devices = lax.axis_size("freq"), lax.axis_size("frame")
    mine, position = lax.axis_index("freq"), lax.axis_index("frame")
    each, chunks, share, depth = GROUP // owners, count // GROUP, bins // devices, devices // 2
    place = jnp.reshape(mine, (1,)).astype(jnp.int32)
    side, level = position & 1, position >> 1
    order = jnp.arange(depth, dtype=jnp.int32)
    keep = (side * depth + (level ^ order)).astype(jnp.int32)
    send = ((side ^ 1) * depth + (level ^ order)).astype(jnp.int32)

    def column(v):
        return jnp.broadcast_to(v[:, None], (v.shape[0], LANES))

    weights = (
        column(norm_gain), w_in.T, column(b_in), w_mid.T, column(b_mid), w_out.T, column(b_out),
    )
    *powers, stacked = prepare(spectra, place, owners, each, chunks)

    modelled = []
    for c in range(chunks):
        pieces = powers[c * owners : (c + 1) * owners]
        pieces = [pieces[0]] + [exchange(pieces[m], "freq", m) for m in range(1, owners)]
        out = model(pieces, place, weights)
        modelled.append([out[0]] + [exchange(out[m], "freq", m) for m in range(1, owners)])

    laid = []
    for c in range(chunks):
        sent = covariance(send, place, stacked, modelled[c], count)
        kept = covariance(keep, place, stacked, modelled[c], count)
        parts = [None] * depth
        for r in list(range(1, depth)) + [0]:
            v = kept[r] + exchange(sent[r], "frame", 1)
            parts[r] = v if r == 0 else exchange(v, "frame", 2 * r)
        laid.append(unpack(parts, count, share))

    mixing = sweep(laid, count, share, frames * devices)
    near = [mixing] + [exchange(mixing, "frame", 2 * r) for r in range(1, depth)]
    far = [exchange(v, "frame", 1) for v in near]
    demixed = apply(jnp.concatenate([keep, send]), jnp.stack(near + far), stacked, count)

    natural = []
    for c in range(chunks):
        for p in range(owners):
            v = modelled[c][0]
            for m in range(1, owners):
                v = jnp.where((mine ^ p) == m, modelled[c][m], v)
            natural.append(v)
    return demixed, jnp.concatenate(natural, axis=0)


def solution(mesh):
    in_specs = (P(None, None, "freq", "frame"), P(), P(), P(), P(), P(), P(), P())
    out_specs = (P(None, None, "freq", "frame"), P(None, "freq", "frame"))
    return jax.shard_map(
        on_device, mesh=mesh, in_specs=in_specs, out_specs=out_specs, check_vma=False
    )
```

```python
import functools

import jax
import jax.numpy as jnp
from jax import lax
from jax.experimental import pallas as pl
from jax.experimental.pallas import tpu as pltpu
from jax.sharding import PartitionSpec as P

epsilon = 1e-05
power_floor = 0.001
variance_floor = 0.25
GROUP = 8
LANES = 128
BF16 = jnp.bfloat16
F32 = jnp.float32
SMEM = pltpu.SMEM
VMEM = pltpu.VMEM


def options(mib=48):
    return pltpu.CompilerParams(vmem_limit_bytes=mib * 1024 * 1024)


def cost(flops, moved, transcendentals=0):
    return pl.CostEstimate(
        flops=int(flops), bytes_accessed=int(moved), transcendentals=int(transcendentals)
    )


def exchange(value, axis, mask):
    size = lax.axis_size(axis)
    return lax.ppermute(value, axis, [(i, i ^ mask) for i in range(size)])


def prepare_kernel(place, x_ref, *refs, owners, each, chunks, count):
    powers, l_ref, rows = refs[:-2], refs[-2], refs[-1]
    mine = place[0]
    bins, frames = x_ref.shape[2], x_ref.shape[3]
    for c in range(chunks):
        for m in range(owners):
            for i in range(each):
                source = c * GROUP + (mine ^ m) * each + i
                re = x_ref[0, source].astype(F32)
                im = x_ref[1, source].astype(F32)
                powers[c * owners + m][i] = jnp.log(re * re + im * im + power_floor).astype(BF16)
    wide = frames // LANES
    pitch = rows.shape[1] // (2 * count)
    for i in range(wide):
        block = x_ref[:, :, :, i * LANES : (i + 1) * LANES].astype(F32)
        block = block.reshape(2 * count, bins, LANES)
        for n in range(2 * count):
            rows[i, n * pitch : n * pitch + bins] = block[n]

    def one(f, carry):
        both = jnp.concatenate(
            [rows[i, pl.ds(f, 2 * count, stride=pitch), :] for i in range(wide)], axis=1
        )
        re, im = both[:count], both[count:]
        upper = jnp.concatenate([re, im], axis=1)
        lower = jnp.concatenate([im, -re], axis=1)
        l_ref[f] = jnp.concatenate([upper, lower], axis=0).astype(BF16)
        return carry

    lax.fori_loop(0, bins, one, 0, unroll=8)


def prepare(spectra, place, owners, each, chunks):
    _, count, bins, frames = spectra.shape
    step = 16
    power = jax.ShapeDtypeStruct((each, bins, frames), BF16)
    shapes = [power] * (chunks * owners)
    shapes.append(jax.ShapeDtypeStruct((bins, 2 * count, 2 * frames), BF16))
    specs = [pl.BlockSpec((each, step, frames), lambda b: (0, b, 0))] * (chunks * owners)
    specs.append(pl.BlockSpec((step, 2 * count, 2 * frames), lambda b: (b, 0, 0)))
    return pl.pallas_call(
        functools.partial(
            prepare_kernel, owners=owners, each=each, chunks=chunks, count=count
        ),
        grid=(bins // step,),
        in_specs=[
            pl.BlockSpec(memory_space=SMEM),
            pl.BlockSpec((2, count, step, frames), lambda b: (0, 0, b, 0)),
        ],
        out_specs=specs,
        out_shape=shapes,
        scratch_shapes=[VMEM((frames // LANES, 2 * count * (step + 8), LANES), F32)],
        compiler_params=options(),
        cost_estimate=cost(20 * spectra.size, 8 * spectra.size, spectra.size // 2),
        name="prepare",
    )(place, spectra)


def silu(v):
    return v / (1.0 + jnp.exp(-v))


def softplus(v):
    return jnp.maximum(v, 0.0) + jnp.log1p(jnp.exp(-jnp.abs(v)))


def model_kernel(place, *refs, owners):
    pieces = refs[:owners]
    gain, w_in, b_in, w_mid, b_mid, w_out, b_out = refs[owners : owners + 7]
    outs = refs[owners + 7 : 2 * owners + 7]
    normed, hidden = refs[2 * owners + 7 :]
    mine = place[0]
    bins, frames = pieces[0].shape[1:]
    total = bins * owners
    wide = frames // LANES

    def spread(column):
        return jnp.concatenate([column] * wide, axis=1)

    values = [piece[0].astype(F32) for piece in pieces]
    average = sum(jnp.sum(v, axis=0, keepdims=True) for v in values) / total
    values = [v - average for v in values]
    square = sum(jnp.sum(v * v, axis=0, keepdims=True) for v in values) / total
    scale = lax.rsqrt(square + epsilon)
    for m in range(owners):
        at = pl.multiple_of((mine ^ m) * bins, bins)
        normed[pl.ds(at, bins), :] = (
            values[m] * scale * spread(gain[pl.ds(at, bins), :])
        ).astype(BF16)

    tile = 256

    def layer(weights, bias, source, target):
        def one(h, carry):
            at = pl.multiple_of(h * tile, tile)
            v = jnp.dot(weights[pl.ds(at, tile), :], source[...], preferred_element_type=F32)
            target[pl.ds(at, tile), :] = silu(v + spread(bias[pl.ds(at, tile), :])).astype(BF16)
            return carry

        lax.fori_loop(0, weights.shape[0] // tile, one, 0, unroll=4)

    layer(w_in, b_in, normed, hidden)
    layer(w_mid, b_mid, hidden, normed)
    for m in range(owners):
        at = pl.multiple_of((mine ^ m) * bins, bins)
        v = jnp.dot(w_out[pl.ds(at, bins), :], normed[...], preferred_element_type=F32)
        outs[m][0] = (softplus(v + spread(b_out[pl.ds(at, bins), :])) + variance_floor).astype(
            BF16
        )


def model(pieces, place, weights):
    owners = len(pieces)
    each, bins, frames = pieces[0].shape
    hidden = weights[1].shape[0]
    block = pl.BlockSpec((1, bins, frames), lambda i: (i, 0, 0))
    whole = [pl.BlockSpec(w.shape, lambda i: (0, 0)) for w in weights]
    return pl.pallas_call(
        functools.partial(model_kernel, owners=owners),
        grid=(each,),
        in_specs=[pl.BlockSpec(memory_space=SMEM)] + [block] * owners + whole,
        out_specs=[block] * owners,
        out_shape=[jax.ShapeDtypeStruct((each, bins, frames), BF16)] * owners,
        scratch_shapes=[VMEM((hidden, frames), BF16), VMEM((hidden, frames), BF16)],
        compiler_params=options(),
        cost_estimate=cost(
            6 * each * hidden * hidden * frames, 6 * hidden * hidden, 8 * each * hidden * frames
        ),
        name="source_model",
    )(place, *pieces, *weights)


def covariance_kernel(table, place, l_ref, *refs, owners, count):
    pieces, (_, o_ref, natural, weight) = refs[:owners], refs[owners:]
    mine = place[0]
    each, bins, frames = pieces[0].shape
    for m in range(owners):
        for i in range(each):
            source = (mine ^ m) * each + i
            natural[source] = pieces[m][i]
            weight[source] = 1.0 / pieces[m][i].astype(F32)
    shape = (count, GROUP * count)
    row = lax.broadcasted_iota(jnp.int32, shape, 0)
    column = lax.rem(lax.broadcasted_iota(jnp.int32, shape, 1), count)
    real = row <= column
    half = bins // 2
    together = min(8, half)

    def weighted(f):
        left = l_ref[f]
        top = left.astype(F32)[:count]
        parts = []
        for j in range(GROUP):
            w = weight[j, pl.ds(f, 1), :]
            parts.append(top * jnp.concatenate([w, w], axis=1))
        right = jnp.concatenate(parts, axis=0)
        high = right.astype(BF16)
        return left, high, (right - high.astype(F32)).astype(BF16)

    def summed(left, high, low):
        dims = (((1,), (1,)), ((), ()))
        v = lax.dot_general(left, high, dims, preferred_element_type=F32)
        v = v + lax.dot_general(left, low, dims, preferred_element_type=F32)
        return jnp.where(real, v[:count], v[count:])

    def some(n, carry):
        first = n * together
        operands = [weighted(first + i + e * half) for i in range(together) for e in range(2)]
        sums = [summed(*o) for o in operands]
        for i in range(together):
            o_ref[0, first + i] = jnp.concatenate([sums[2 * i], sums[2 * i + 1]], axis=1)
        return carry

    lax.fori_loop(0, half // together, some, 0)


def covariance(table, place, stacked, pieces, natural, chunk, count):
    owners, shares = len(pieces), table.shape[0]
    each, bins, frames = pieces[0].shape
    share = stacked.shape[0] // lax.axis_size("frame")
    piece = pl.BlockSpec((each, share, frames), lambda r, table, place: (0, table[r], 0))
    lanes = 2 * GROUP * count
    return pl.pallas_call(
        functools.partial(covariance_kernel, owners=owners, count=count),
        grid_spec=pltpu.PrefetchScalarGridSpec(
            num_scalar_prefetch=2,
            grid=(shares,),
            in_specs=[
                pl.BlockSpec(
                    (share,) + stacked.shape[1:], lambda r, table, place: (table[r], 0, 0)
                )
            ]
            + [piece] * owners
            + [pl.BlockSpec(memory_space=pl.ANY)],
            out_specs=[
                pl.BlockSpec(
                    (1, share // 2, count, lanes), lambda r, table, place: (r, 0, 0, 0)
                ),
                pl.BlockSpec(
                    (GROUP, share, frames), lambda r, table, place: (chunk, table[r], 0)
                ),
            ],
            scratch_shapes=[VMEM((GROUP, share, frames), F32)],
        ),
        out_shape=[
            jax.ShapeDtypeStruct((shares, share // 2, count, lanes), F32),
            jax.ShapeDtypeStruct((count, bins, frames), BF16),
        ],
        input_output_aliases={} if natural.shape[0] != count else {3 + owners: 1},
        compiler_params=options(),
        cost_estimate=cost(
            shares * share * 8 * count * count * GROUP * frames * 2,
            shares * share * (8 * count * frames + 4 * count * count * GROUP),
        ),
        name="covariance",
    )(table, place, stacked, *pieces, natural)


def unpack_kernel(*refs, count, share, lanes_b):
    parts, o_ref, turned = refs[:-2], refs[-2], refs[-1]
    half = GROUP * count
    blocks = o_ref.shape[1]

    def turn(a, carry):
        v = parts[0][:, a, :]
        for part in parts[1:]:
            v = v + part[:, a, :]
        v = jnp.concatenate([v[:, :half], v[:, half:]], axis=0)
        turned[a, :, 0:share] = v.T
        return carry

    lax.fori_loop(0, count, turn, 0, unroll=8)

    def lay(a, carry):
        for g in range(blocks):
            re, im = [], []
            for i in range(lanes_b):
                b = g * lanes_b + i
                if b >= count:
                    re.append(jnp.zeros((GROUP, share), F32))
                    im.append(jnp.zeros((GROUP, share), F32))
                    continue
                low, high = jnp.minimum(a, b), jnp.maximum(a, b)
                sign = jnp.where(a > b, 1.0, jnp.where(a < b, -1.0, 0.0))
                re.append(turned[low, pl.ds(high, GROUP, stride=count), :][:, :share])
                im.append(turned[high, pl.ds(low, GROUP, stride=count), :][:, :share] * sign)
            o_ref[a, g, 0] = jnp.concatenate(re, axis=1)
            o_ref[a, g, 1] = jnp.concatenate(im, axis=1)
        return carry

    lax.fori_loop(0, count, lay, 0, unroll=4)


def unpack(parts, count, share):
    lanes_b = LANES // share
    blocks = -(-count // lanes_b)
    shape = (count, blocks, 2, GROUP, LANES)
    return pl.pallas_call(
        functools.partial(unpack_kernel, count=count, share=share, lanes_b=lanes_b),
        out_shape=jax.ShapeDtypeStruct(shape, F32),
        scratch_shapes=[VMEM((count, GROUP * count, LANES), F32)],
        compiler_params=options(),
        cost_estimate=cost(10 * parts[0].size, 4 * parts[0].size * (len(parts) + 2)),
        name="unpack",
    )(*parts)


def sweep_kernel(*refs, count, share, frames):
    chunks = count // GROUP
    v_refs, o_ref, wr, wi, diagonal, flat = refs[:chunks], *refs[chunks:]
    lanes_b = LANES // share
    blocks = v_refs[0].shape[1]
    full = (GROUP, LANES)
    sub = lax.broadcasted_iota(jnp.int32, full, 0)
    lane = lax.broadcasted_iota(jnp.int32, full, 1)
    group = [(lane >= i * share) & (lane < (i + 1) * share) for i in range(lanes_b)]
    zero = jnp.zeros(full, F32)

    def start(a, carry):
        for c in range(chunks):
            wr[a, c] = jnp.where(sub + c * GROUP == a, 1.0, 0.0)
            wi[a, c] = zero
        return carry

    lax.fori_loop(0, count, start, 0)
    for c in range(chunks):
        for g in range(blocks):
            for part in range(2):
                d = zero
                for s in range(GROUP):
                    d = jnp.where(sub == s, v_refs[c][c * GROUP + s, g, part], d)
                diagonal[c, g, part] = d

    def total(x):
        shift = share
        while shift < LANES:
            x = x + pltpu.roll(x, shift, 1)
            shift *= 2
        return x

    for k in range(count):
        ck, sk = divmod(k, GROUP)
        used = k // lanes_b + 1
        pick_r, pick_i = [], []
        for g in range(used):
            pr, pi = zero, zero
            for i in range(lanes_b):
                b = g * lanes_b + i
                if b <= k:
                    pr = jnp.where(group[i], wr[b, ck, sk : sk + 1, :], pr)
                    pi = jnp.where(group[i], wi[b, ck, sk : sk + 1, :], pi)
            pick_r.append(pr)
            pick_i.append(pi)

        def product(load):
            ur, ui = zero, zero
            for g in range(used):
                vr, vi = load(g, 0), load(g, 1)
                ur = ur + vr * pick_r[g] + vi * pick_i[g]
                ui = ui + vi * pick_r[g] - vr * pick_i[g]
            return ur, ui

        def gather(a, carry):
            out = []
            kr = wr[a, ck, sk : sk + 1, :]
            ki = wi[a, ck, sk : sk + 1, :]
            for c in range(chunks):
                nr, ni, de = carry[3 * c : 3 * c + 3]
                ur, ui = product(lambda g, part: v_refs[c][a, g, part])
                ar, ai = wr[a, c], wi[a, c]
                out.append(nr + ar * ur - ai * ui)
                out.append(ni + ar * ui + ai * ur)
                out.append(de + kr * ur - ki * ui)
            return tuple(out)

        sums = lax.fori_loop(0, k + 1, gather, (zero,) * (3 * chunks), unroll=min(2, k + 1))
        steer = []
        for c in range(chunks):
            nr, ni, de = sums[3 * c : 3 * c + 3]
            if (c + 1) * GROUP > k + 1:
                ur, ui = product(lambda g, part: diagonal[c, g, part])
                later = sub + c * GROUP > k
                nr = nr + jnp.where(later, ur, 0.0)
                ni = ni + jnp.where(later, ui, 0.0)
            nr, ni, de = total(nr), total(ni), total(de)
            inverse = 1.0 / de
            vr, vi = nr * inverse, ni * inverse
            if c == ck:
                vr = jnp.where(sub == sk, 1.0 - lax.rsqrt(de / frames), vr)
                vi = jnp.where(sub == sk, 0.0, vi)
            steer.append((vr, vi))

        def update(a, carry):
            kr = jnp.broadcast_to(wr[a, ck, sk : sk + 1, :], full)
            ki = jnp.broadcast_to(wi[a, ck, sk : sk + 1, :], full)
            for c in range(chunks):
                vr, vi = steer[c]
                wr[a, c] = wr[a, c] - (vr * kr - vi * ki)
                wi[a, c] = wi[a, c] - (vr * ki + vi * kr)
            return carry

        lax.fori_loop(0, k + 1, update, 0, unroll=min(2, k + 1))

    def pack(a, carry):
        for c in range(chunks):
            at = c * GROUP * 2 * count + a
            flat[pl.ds(at, GROUP, stride=2 * count), :] = wr[a, c]
            flat[pl.ds(at + count, GROUP, stride=2 * count), :] = -wi[a, c]
        return carry

    lax.fori_loop(0, count, pack, 0)
    for i in range(flat.shape[0] // LANES):
        o_ref[:, i * LANES : (i + 1) * LANES] = flat[i * LANES : (i + 1) * LANES, :].T[:share]


def sweep(parts, count, share, frames):
    chunks = count // GROUP
    blocks = parts[0].shape[1]
    state = VMEM((count, chunks, GROUP, LANES), F32)
    return pl.pallas_call(
        functools.partial(sweep_kernel, count=count, share=share, frames=frames),
        out_shape=jax.ShapeDtypeStruct((share, 2 * count * count), F32),
        scratch_shapes=[
            state,
            state,
            VMEM((chunks, blocks, 2, GROUP, LANES), F32),
            VMEM((2 * count * count, LANES), F32),
        ],
        compiler_params=options(),
        cost_estimate=cost(4500 * count**3, 4 * 3 * parts[0].size),
        name="sweep",
    )(*parts)


def apply_kernel(table, w_ref, l_ref, o_ref, mixing, rows, *, count):
    share = w_ref.shape[1]
    frames = o_ref.shape[3]
    wide = 2 * count
    tiles = frames // LANES
    pitch = share + 8
    pad = jnp.zeros((share, LANES - wide), F32)
    for j in range(count):
        v = jnp.concatenate([w_ref[0, :, j * wide : (j + 1) * wide], pad], axis=1)
        mixing[pl.ds(j, share, stride=count), :] = v

    def one(f, carry):
        at = pl.multiple_of(f * count, count)
        w = mixing[pl.ds(at, count), 0:wide]
        high = w.astype(BF16).astype(F32)
        middle = (w - high).astype(BF16).astype(F32)
        low = w - high - middle
        left = jnp.concatenate([high, middle, low], axis=0).astype(BF16)
        y = jnp.dot(left, l_ref[f], preferred_element_type=F32)
        y = y[:count] + (y[count : 2 * count] + y[2 * count :])
        for c in range(2):
            for i in range(tiles):
                v = y[:, c * frames + i * LANES : c * frames + (i + 1) * LANES]
                rows[i, pl.ds(c * count * pitch + f, count, stride=pitch), :] = v
        return carry

    lax.fori_loop(0, share, one, 0, unroll=8)
    for i in range(tiles):
        v = rows[i].reshape(2, count, pitch, LANES)[:, :, :share]
        o_ref[:, :, :, i * LANES : (i + 1) * LANES] = v


def apply(table, mixing, stacked, count):
    shares, share = mixing.shape[:2]
    bins, frames = stacked.shape[0], stacked.shape[2] // 2
    return pl.pallas_call(
        functools.partial(apply_kernel, count=count),
        grid_spec=pltpu.PrefetchScalarGridSpec(
            num_scalar_prefetch=1,
            grid=(shares,),
            in_specs=[
                pl.BlockSpec((1,) + mixing.shape[1:], lambda r, table: (r, 0, 0)),
                pl.BlockSpec((share,) + stacked.shape[1:], lambda r, table: (table[r], 0, 0)),
            ],
            out_specs=pl.BlockSpec(
                (2, count, share, frames), lambda r, table: (0, 0, table[r], 0)
            ),
            scratch_shapes=[
                VMEM((share * count, LANES), F32),
                VMEM((frames // LANES, 2 * count * (share + 8), LANES), F32),
            ],
        ),
        out_shape=jax.ShapeDtypeStruct((2, count, bins, frames), F32),
        compiler_params=options(),
        cost_estimate=cost(
            16 * count * count * bins * frames, stacked.size * 2 + 8 * count * bins * frames
        ),
        name="apply",
    )(table, mixing, stacked)


def on_device(spectra, norm_gain, w_in, b_in, w_mid, b_mid, w_out, b_out):
    _, count, bins, frames = spectra.shape
    owners, devices = lax.axis_size("freq"), lax.axis_size("frame")
    mine, position = lax.axis_index("freq"), lax.axis_index("frame")
    each, chunks, share, depth = GROUP // owners, count // GROUP, bins // devices, devices // 2
    place = jnp.reshape(mine, (1,)).astype(jnp.int32)
    side, level = position & 1, position >> 1
    order = jnp.arange(depth, dtype=jnp.int32)
    keep = (side * depth + (level ^ order)).astype(jnp.int32)
    send = ((side ^ 1) * depth + (level ^ order)).astype(jnp.int32)

    def column(v):
        return jnp.broadcast_to(v[:, None], (v.shape[0], LANES))

    weights = (
        column(norm_gain), w_in.T, column(b_in), w_mid.T, column(b_mid), w_out.T, column(b_out),
    )
    *powers, stacked = prepare(spectra, place, owners, each, chunks)

    modelled = []
    for c in range(chunks):
        pieces = powers[c * owners : (c + 1) * owners]
        pieces = [pieces[0]] + [exchange(pieces[m], "freq", m) for m in range(1, owners)]
        out = model(pieces, place, weights)
        modelled.append([out[0]] + [exchange(out[m], "freq", m) for m in range(1, owners)])

    laid = []
    variances = place
    for c in range(chunks):
        sent, variances = covariance(send, place, stacked, modelled[c], variances, c, count)
        kept, variances = covariance(keep, place, stacked, modelled[c], variances, c, count)
        parts = [None] * depth
        for r in list(range(1, depth)) + [0]:
            v = kept[r] + exchange(sent[r], "frame", 1)
            parts[r] = v if r == 0 else exchange(v, "frame", 2 * r)
        laid.append(unpack(parts, count, share))

    mixing = sweep(laid, count, share, frames * devices)
    near = [mixing] + [exchange(mixing, "frame", 2 * r) for r in range(1, depth)]
    far = [exchange(v, "frame", 1) for v in near]
    demixed = apply(jnp.concatenate([keep, send]), jnp.stack(near + far), stacked, count)

    return demixed, variances


def solution(mesh):
    in_specs = (P(None, None, "freq", "frame"), P(), P(), P(), P(), P(), P(), P())
    out_specs = (P(None, None, "freq", "frame"), P(None, "freq", "frame"))
    return jax.shard_map(
        on_device, mesh=mesh, in_specs=in_specs, out_specs=out_specs, check_vma=False
    )
```

```python
import functools

import jax
import jax.numpy as jnp
from jax import lax
from jax.experimental import pallas as pl
from jax.experimental.pallas import tpu as pltpu
from jax.sharding import PartitionSpec as P

epsilon = 1e-05
power_floor = 0.001
variance_floor = 0.25
ridge = 2.0**-14
floor = 1e-8
GROUP = 8
LANES = 128
BF16 = jnp.bfloat16
F32 = jnp.float32
SMEM = pltpu.SMEM
VMEM = pltpu.VMEM


def options(mib=48):
    return pltpu.CompilerParams(vmem_limit_bytes=mib * 1024 * 1024)


def cost(flops, moved, transcendentals=0):
    return pl.CostEstimate(
        flops=int(flops), bytes_accessed=int(moved), transcendentals=int(transcendentals)
    )


def exchange(value, axis, mask):
    size = lax.axis_size(axis)
    return lax.ppermute(value, axis, [(i, i ^ mask) for i in range(size)])


def prepare_kernel(place, x_ref, *refs, owners, each, chunks, count):
    powers, l_ref, rows = refs[:-2], refs[-2], refs[-1]
    mine = place[0]
    bins, frames = x_ref.shape[2], x_ref.shape[3]
    for c in range(chunks):
        for m in range(owners):
            for i in range(each):
                source = c * GROUP + (mine ^ m) * each + i
                re = x_ref[0, source].astype(F32)
                im = x_ref[1, source].astype(F32)
                powers[c * owners + m][i] = jnp.log(re * re + im * im + power_floor).astype(BF16)
    wide = frames // LANES
    pitch = rows.shape[1] // (2 * count)
    for i in range(wide):
        block = x_ref[:, :, :, i * LANES : (i + 1) * LANES].astype(F32)
        block = block.reshape(2 * count, bins, LANES)
        for n in range(2 * count):
            rows[i, n * pitch : n * pitch + bins] = block[n]

    def one(f, carry):
        both = jnp.concatenate(
            [rows[i, pl.ds(f, 2 * count, stride=pitch), :] for i in range(wide)], axis=1
        )
        re, im = both[:count], both[count:]
        upper = jnp.concatenate([re, im], axis=1)
        lower = jnp.concatenate([im, -re], axis=1)
        l_ref[f] = jnp.concatenate([upper, lower], axis=0).astype(BF16)
        return carry

    lax.fori_loop(0, bins, one, 0, unroll=8)


def prepare(spectra, place, owners, each, chunks):
    _, count, bins, frames = spectra.shape
    step = 16
    power = jax.ShapeDtypeStruct((each, bins, frames), BF16)
    shapes = [power] * (chunks * owners)
    shapes.append(jax.ShapeDtypeStruct((bins, 2 * count, 2 * frames), BF16))
    specs = [pl.BlockSpec((each, step, frames), lambda b: (0, b, 0))] * (chunks * owners)
    specs.append(pl.BlockSpec((step, 2 * count, 2 * frames), lambda b: (b, 0, 0)))
    return pl.pallas_call(
        functools.partial(
            prepare_kernel, owners=owners, each=each, chunks=chunks, count=count
        ),
        grid=(bins // step,),
        in_specs=[
            pl.BlockSpec(memory_space=SMEM),
            pl.BlockSpec((2, count, step, frames), lambda b: (0, 0, b, 0)),
        ],
        out_specs=specs,
        out_shape=shapes,
        scratch_shapes=[VMEM((frames // LANES, 2 * count * (step + 8), LANES), F32)],
        compiler_params=options(),
        cost_estimate=cost(20 * spectra.size, 8 * spectra.size, spectra.size // 2),
        name="prepare",
    )(place, spectra)


def silu(v):
    return v / (1.0 + jnp.exp(-v))


def softplus(v):
    return jnp.maximum(v, 0.0) + jnp.log1p(jnp.exp(-jnp.abs(v)))


def model_kernel(place, *refs, owners):
    pieces = refs[:owners]
    gain, w_in, b_in, w_mid, b_mid, w_out, b_out = refs[owners : owners + 7]
    outs = refs[owners + 7 : 2 * owners + 7]
    normed, hidden = refs[2 * owners + 7 :]
    mine = place[0]
    bins, frames = pieces[0].shape[1:]
    total = bins * owners
    wide = frames // LANES

    def spread(column):
        return jnp.concatenate([column] * wide, axis=1)

    values = [piece[0].astype(F32) for piece in pieces]
    average = sum(jnp.sum(v, axis=0, keepdims=True) for v in values) / total
    values = [v - average for v in values]
    square = sum(jnp.sum(v * v, axis=0, keepdims=True) for v in values) / total
    scale = lax.rsqrt(square + epsilon)
    for m in range(owners):
        at = pl.multiple_of((mine ^ m) * bins, bins)
        normed[pl.ds(at, bins), :] = (
            values[m] * scale * spread(gain[pl.ds(at, bins), :])
        ).astype(BF16)

    tile = 256

    def layer(weights, bias, source, target):
        def one(h, carry):
            at = pl.multiple_of(h * tile, tile)
            v = jnp.dot(weights[pl.ds(at, tile), :], source[...], preferred_element_type=F32)
            target[pl.ds(at, tile), :] = silu(v + spread(bias[pl.ds(at, tile), :])).astype(BF16)
            return carry

        lax.fori_loop(0, weights.shape[0] // tile, one, 0, unroll=4)

    layer(w_in, b_in, normed, hidden)
    layer(w_mid, b_mid, hidden, normed)
    for m in range(owners):
        at = pl.multiple_of((mine ^ m) * bins, bins)
        v = jnp.dot(w_out[pl.ds(at, bins), :], normed[...], preferred_element_type=F32)
        outs[m][0] = (softplus(v + spread(b_out[pl.ds(at, bins), :])) + variance_floor).astype(
            BF16
        )


def model(pieces, place, weights):
    owners = len(pieces)
    each, bins, frames = pieces[0].shape
    hidden = weights[1].shape[0]
    block = pl.BlockSpec((1, bins, frames), lambda i: (i, 0, 0))
    whole = [pl.BlockSpec(w.shape, lambda i: (0, 0)) for w in weights]
    return pl.pallas_call(
        functools.partial(model_kernel, owners=owners),
        grid=(each,),
        in_specs=[pl.BlockSpec(memory_space=SMEM)] + [block] * owners + whole,
        out_specs=[block] * owners,
        out_shape=[jax.ShapeDtypeStruct((each, bins, frames), BF16)] * owners,
        scratch_shapes=[VMEM((hidden, frames), BF16), VMEM((hidden, frames), BF16)],
        compiler_params=options(),
        cost_estimate=cost(
            6 * each * hidden * hidden * frames, 6 * hidden * hidden, 8 * each * hidden * frames
        ),
        name="source_model",
    )(place, *pieces, *weights)


def covariance_kernel(table, place, l_ref, *refs, owners, count):
    pieces, (_, o_ref, natural, weight) = refs[:owners], refs[owners:]
    mine = place[0]
    each, bins, frames = pieces[0].shape
    for m in range(owners):
        for i in range(each):
            source = (mine ^ m) * each + i
            natural[source] = pieces[m][i]
            weight[source] = 1.0 / pieces[m][i].astype(F32)
    shape = (count, GROUP * count)
    row = lax.broadcasted_iota(jnp.int32, shape, 0)
    column = lax.rem(lax.broadcasted_iota(jnp.int32, shape, 1), count)
    real = row <= column
    quarter = bins // 4
    together = min(4, quarter)

    def weighted(f):
        left = l_ref[f]
        top = left.astype(F32)[:count]
        parts = []
        for j in range(GROUP):
            w = weight[j, pl.ds(f, 1), :]
            parts.append(top * jnp.concatenate([w, w], axis=1))
        return left, jnp.concatenate(parts, axis=0).astype(BF16)

    def summed(left, right):
        dims = (((1,), (1,)), ((), ()))
        v = lax.dot_general(left, right, dims, preferred_element_type=F32)
        return jnp.where(real, v[:count], v[count:])

    def some(n, carry):
        first = n * together
        operands = [weighted(first + i + e * quarter) for i in range(together) for e in range(4)]
        sums = [summed(*o) for o in operands]
        for i in range(together):
            v = sums[4 * i : 4 * i + 4]
            rows = [jnp.concatenate([v[e], v[e + 2]], axis=1) for e in range(2)]
            o_ref[0, first + i] = jnp.concatenate(rows, axis=0).astype(o_ref.dtype)
        return carry

    lax.fori_loop(0, quarter // together, some, 0)


def covariance(table, place, stacked, pieces, natural, chunk, count, held):
    owners, shares = len(pieces), table.shape[0]
    each, bins, frames = pieces[0].shape
    share = stacked.shape[0] // lax.axis_size("frame")
    piece = pl.BlockSpec((each, share, frames), lambda r, table, place: (0, table[r], 0))
    lanes = 2 * GROUP * count
    return pl.pallas_call(
        functools.partial(covariance_kernel, owners=owners, count=count),
        grid_spec=pltpu.PrefetchScalarGridSpec(
            num_scalar_prefetch=2,
            grid=(shares,),
            in_specs=[
                pl.BlockSpec(
                    (share,) + stacked.shape[1:], lambda r, table, place: (table[r], 0, 0)
                )
            ]
            + [piece] * owners
            + [pl.BlockSpec(memory_space=pl.ANY)],
            out_specs=[
                pl.BlockSpec(
                    (1, share // 4, 2 * count, lanes), lambda r, table, place: (r, 0, 0, 0)
                ),
                pl.BlockSpec(
                    (GROUP, share, frames), lambda r, table, place: (chunk, table[r], 0)
                ),
            ],
            scratch_shapes=[VMEM((GROUP, share, frames), F32)],
        ),
        out_shape=[
            jax.ShapeDtypeStruct((shares, share // 4, 2 * count, lanes), held),
            jax.ShapeDtypeStruct((count, bins, frames), BF16),
        ],
        input_output_aliases={} if natural.shape[0] != count else {3 + owners: 1},
        compiler_params=options(),
        cost_estimate=cost(
            shares * share * 8 * count * count * GROUP * frames * 2,
            shares * share * (8 * count * frames + 4 * count * count * GROUP),
        ),
        name="covariance",
    )(table, place, stacked, *pieces, natural)


def unpack_kernel(*refs, count, share, lanes_b):
    parts, o_ref, added, turned = refs[:-3], refs[-3], refs[-2], refs[-1]
    half = GROUP * count
    blocks = o_ref.shape[1]

    v = parts[0][...].astype(F32)
    for part in parts[1:]:
        v = v + part[...].astype(F32)
    added[...] = v

    def turn(a, carry):
        v, w = added[:, a, :], added[:, count + a, :]
        v = jnp.concatenate([v[:, :half], w[:, :half], v[:, half:], w[:, half:]], axis=0)
        turned[a, :, 0:share] = v.T
        return carry

    lax.fori_loop(0, count, turn, 0, unroll=8)

    def lay(a, carry):
        for g in range(blocks):
            re, im = [], []
            for i in range(lanes_b):
                b = g * lanes_b + i
                if b >= count:
                    re.append(jnp.zeros((GROUP, share), F32))
                    im.append(jnp.zeros((GROUP, share), F32))
                    continue
                low, high = jnp.minimum(a, b), jnp.maximum(a, b)
                sign = jnp.where(a > b, 1.0, jnp.where(a < b, -1.0, 0.0))
                re.append(turned[low, pl.ds(high, GROUP, stride=count), :][:, :share])
                im.append(turned[high, pl.ds(low, GROUP, stride=count), :][:, :share] * sign)
            o_ref[a, g, 0] = jnp.concatenate(re, axis=1)
            o_ref[a, g, 1] = jnp.concatenate(im, axis=1)
        return carry

    lax.fori_loop(0, count, lay, 0, unroll=4)


def unpack(parts, count, share):
    lanes_b = LANES // share
    blocks = -(-count // lanes_b)
    shape = (count, blocks, 2, GROUP, LANES)
    return pl.pallas_call(
        functools.partial(unpack_kernel, count=count, share=share, lanes_b=lanes_b),
        out_shape=jax.ShapeDtypeStruct(shape, F32),
        scratch_shapes=[VMEM(parts[0].shape, F32), VMEM((count, GROUP * count, LANES), F32)],
        compiler_params=options(),
        cost_estimate=cost(10 * parts[0].size, 4 * parts[0].size * (len(parts) + 2)),
        name="unpack",
    )(*parts)


def sweep_kernel(*refs, count, share, frames):
    chunks = count // GROUP
    v_refs = refs[:chunks]
    factor, inverse_ref, o_ref, wr, wi, diagonal, flat = refs[chunks:]
    lanes_b = LANES // share
    blocks = v_refs[0].shape[1]
    full = (GROUP, LANES)
    sub = lax.broadcasted_iota(jnp.int32, full, 0)
    lane = lax.broadcasted_iota(jnp.int32, full, 1)
    group = [(lane >= i * share) & (lane < (i + 1) * share) for i in range(lanes_b)]
    zero = jnp.zeros(full, F32)

    wr[...] = jnp.zeros_like(wr)
    wi[...] = jnp.zeros_like(wi)
    for c in range(chunks):
        for g in range(blocks):

            def own(a, carry):
                lr, li = factor[a, 0, c], factor[a, 1, c]
                vr, vi = v_refs[c][a, g, 0], v_refs[c][a, g, 1]
                return carry[0] + lr * vr - li * vi, carry[1] + lr * vi + li * vr

            first = lax.fori_loop(0, (c + 1) * GROUP, own, (zero, zero), unroll=4)
            diagonal[c, g, 0], diagonal[c, g, 1] = first

    def total(x):
        shift = share
        while shift < LANES:
            x = x + pltpu.roll(x, shift, 1)
            shift *= 2
        return x

    for k in range(count):
        ck, sk = divmod(k, GROUP)
        used = k // lanes_b + 1
        for a in range(k + 1):
            wr[a, ck] = wr[a, ck] + jnp.where(sub == sk, factor[a, 0, ck], 0.0)
            wi[a, ck] = wi[a, ck] + jnp.where(sub == sk, factor[a, 1, ck], 0.0)
        pick_r, pick_i = [], []
        for g in range(used):
            pr, pi = zero, zero
            for i in range(lanes_b):
                b = g * lanes_b + i
                if b <= k:
                    pr = jnp.where(group[i], wr[b, ck, sk : sk + 1, :], pr)
                    pi = jnp.where(group[i], wi[b, ck, sk : sk + 1, :], pi)
            pick_r.append(pr)
            pick_i.append(pi)

        def product(load):
            ur, ui = zero, zero
            for g in range(used):
                vr, vi = load(g, 0), load(g, 1)
                ur = ur + vr * pick_r[g] + vi * pick_i[g]
                ui = ui + vi * pick_r[g] - vr * pick_i[g]
            return ur, ui

        def gather(a, carry):
            out = []
            kr = wr[a, ck, sk : sk + 1, :]
            ki = wi[a, ck, sk : sk + 1, :]
            for c in range(chunks):
                nr, ni, de = carry[3 * c : 3 * c + 3]
                ur, ui = product(lambda g, part: v_refs[c][a, g, part])
                ar, ai = wr[a, c], wi[a, c]
                out.append(nr + ar * ur - ai * ui)
                out.append(ni + ar * ui + ai * ur)
                out.append(de + kr * ur - ki * ui)
            return tuple(out)

        sums = lax.fori_loop(0, k + 1, gather, (zero,) * (3 * chunks), unroll=min(2, k + 1))
        steer = []
        for c in range(chunks):
            nr, ni, de = sums[3 * c : 3 * c + 3]
            if (c + 1) * GROUP > k + 1:
                ur, ui = product(lambda g, part: diagonal[c, g, part])
                later = sub + c * GROUP > k
                nr = nr + jnp.where(later, ur, 0.0)
                ni = ni + jnp.where(later, ui, 0.0)
            nr, ni, de = total(nr), total(ni), total(de)
            inverse = 1.0 / de
            vr, vi = nr * inverse, ni * inverse
            if c == ck:
                vr = jnp.where(sub == sk, 1.0 - lax.rsqrt(de / frames), vr)
                vi = jnp.where(sub == sk, 0.0, vi)
            steer.append((vr, vi))

        def update(a, carry):
            kr = jnp.broadcast_to(wr[a, ck, sk : sk + 1, :], full)
            ki = jnp.broadcast_to(wi[a, ck, sk : sk + 1, :], full)
            for c in range(chunks):
                vr, vi = steer[c]
                wr[a, c] = wr[a, c] - (vr * kr - vi * ki)
                wi[a, c] = wi[a, c] - (vr * ki + vi * kr)
            return carry

        lax.fori_loop(0, k + 1, update, 0, unroll=min(2, k + 1))

    for a in range(count):

        def product(b, carry):
            tr = inverse_ref[a, 0, pl.ds(b, 1), :]
            ti = inverse_ref[a, 1, pl.ds(b, 1), :]
            out = []
            for c in range(chunks):
                r, i = wr[b, c], wi[b, c]
                out.append(carry[2 * c] + r * tr - i * ti)
                out.append(carry[2 * c + 1] + r * ti + i * tr)
            return tuple(out)

        sums = lax.fori_loop(a, count, product, (zero,) * (2 * chunks), unroll=min(4, count - a))
        for c in range(chunks):
            at = c * GROUP * 2 * count + a
            flat[pl.ds(at, GROUP, stride=2 * count), :] = sums[2 * c]
            flat[pl.ds(at + count, GROUP, stride=2 * count), :] = -sums[2 * c + 1]
    flatten(flat, o_ref, share)


def flatten(flat, o_ref, share):
    for i in range(flat.shape[0] // LANES):
        o_ref[:, i * LANES : (i + 1) * LANES] = flat[i * LANES : (i + 1) * LANES, :].T[:share]


def whiten_kernel(table, l_ref, factor, inverse_ref, o_ref, raw, ar, ai, flat, *, count, frames):
    share = l_ref.shape[0]
    chunks = count // GROUP
    wide = 2 * count
    copies = LANES // share
    dims = (((1,), (1,)), ((), ()))

    def sums(f, carry):
        left = l_ref[f]
        v = lax.dot_general(left, left, dims, preferred_element_type=F32)
        at = pl.multiple_of(f * wide, wide)
        pad = jnp.zeros((wide, LANES - wide), F32)
        raw[pl.ds(at, wide), :] = jnp.concatenate([v * (1.0 / frames), pad], axis=1)
        return carry

    lax.fori_loop(0, share, sums, 0, unroll=8)

    def turn(a, carry):
        re = raw[pl.ds(a, share, stride=wide), :].T[:count]
        im = raw[pl.ds(count + a, share, stride=wide), :].T[:count]
        ar[a] = jnp.concatenate([re] * copies, axis=1)
        ai[a] = jnp.concatenate([-im] * copies, axis=1)
        return carry

    lax.fori_loop(0, count, turn, 0, unroll=4)
    row = lax.broadcasted_iota(jnp.int32, (count, LANES), 0)
    zero = jnp.zeros((count, LANES), F32)

    def begin(a, carry):
        inverse_ref[a, 0] = jnp.where(row == a, 1.0, 0.0)
        inverse_ref[a, 1] = zero
        ar[a] = ar[a] + jnp.where(row == a, ar[a] * ridge + floor, 0.0)
        return carry

    lax.fori_loop(0, count, begin, 0, unroll=4)
    for k in range(count):
        scale = lax.rsqrt(ar[k, k : k + 1, :])
        lr = jnp.where(row >= k, ar[k] * scale, 0.0)
        li = jnp.where(row > k, ai[k] * scale, 0.0)
        for c in range(chunks):
            factor[k, 0, c] = lr[c * GROUP : (c + 1) * GROUP]
            factor[k, 1, c] = li[c * GROUP : (c + 1) * GROUP]
        ar[k], ai[k] = lr, li

        def right(b, carry):
            br, bi = ar[k, pl.ds(b, 1), :], ai[k, pl.ds(b, 1), :]
            ar[b] = ar[b] - (lr * br + li * bi)
            ai[b] = ai[b] - (li * br - lr * bi)
            return carry

        if k + 1 < count:
            lax.fori_loop(k + 1, count, right, 0, unroll=min(2, count - k - 1))

        def left(b, carry):
            tr = inverse_ref[b, 0, k : k + 1, :] * scale
            ti = inverse_ref[b, 1, k : k + 1, :] * scale
            r, i = inverse_ref[b, 0], inverse_ref[b, 1]
            nr, ni = r - (lr * tr - li * ti), i - (lr * ti + li * tr)
            inverse_ref[b, 0] = jnp.where(row == k, tr, nr)
            inverse_ref[b, 1] = jnp.where(row == k, ti, ni)
            return carry

        lax.fori_loop(0, k + 1, left, 0, unroll=min(2, k + 1))
    for a in range(count):
        for c in range(chunks):
            at = c * GROUP * wide + a
            rows = slice(c * GROUP, (c + 1) * GROUP)
            flat[pl.ds(at, GROUP, stride=wide), :] = inverse_ref[a, 0, rows, :]
            flat[pl.ds(at + count, GROUP, stride=wide), :] = -inverse_ref[a, 1, rows, :]
    flatten(flat, o_ref, share)


def whiten(table, stacked, count, share):
    wide, frames = 2 * count, stacked.shape[2] // 2
    shapes = [
        (count, 2, count // GROUP, GROUP, LANES),
        (count, 2, count, LANES),
        (share, wide * count),
    ]
    state = VMEM((count, count, LANES), F32)
    return pl.pallas_call(
        functools.partial(whiten_kernel, count=count, frames=frames),
        grid_spec=pltpu.PrefetchScalarGridSpec(
            num_scalar_prefetch=1,
            grid=(1,),
            in_specs=[
                pl.BlockSpec((share,) + stacked.shape[1:], lambda r, table: (table[0], 0, 0))
            ],
            out_specs=[
                pl.BlockSpec(x, functools.partial(lambda n, r, table: (0,) * n, len(x)))
                for x in shapes
            ],
            scratch_shapes=[
                VMEM((share * wide, LANES), F32), state, state, VMEM((wide * count, LANES), F32),
            ],
        ),
        out_shape=[jax.ShapeDtypeStruct(x, F32) for x in shapes],
        compiler_params=options(),
        cost_estimate=cost(3000 * count**3, share * stacked.shape[1] * stacked.shape[2] * 2),
        name="whiten",
    )(table, stacked)


def sweep(parts, factor, inverse, count, share, frames):
    chunks = count // GROUP
    blocks = parts[0].shape[1]
    state = VMEM((count, chunks, GROUP, LANES), F32)
    return pl.pallas_call(
        functools.partial(sweep_kernel, count=count, share=share, frames=frames),
        out_shape=jax.ShapeDtypeStruct((share, 2 * count * count), F32),
        scratch_shapes=[
            state,
            state,
            VMEM((chunks, blocks, 2, GROUP, LANES), F32),
            VMEM((2 * count * count, LANES), F32),
        ],
        compiler_params=options(),
        cost_estimate=cost(4500 * count**3, 4 * 3 * parts[0].size),
        name="sweep",
    )(*parts, factor, inverse)


def apply_kernel(table, w_ref, l_ref, o_ref, mixing, *rows, count, spectra):
    share = w_ref.shape[1]
    frames = l_ref.shape[2] // 2
    wide = 2 * count
    tiles = frames // LANES
    pitch = share + 8
    pad = jnp.zeros((share, LANES - wide), F32)
    for j in range(count):
        v = jnp.concatenate([w_ref[0, :, j * wide : (j + 1) * wide], pad], axis=1)
        mixing[pl.ds(j, share, stride=count), :] = v

    def one(f, carry):
        at = pl.multiple_of(f * count, count)
        w = mixing[pl.ds(at, count), 0:wide]
        high = w.astype(BF16).astype(F32)
        middle = (w - high).astype(BF16).astype(F32)
        low = w - high - middle
        left = jnp.concatenate([high, middle, low], axis=0).astype(BF16)
        y = jnp.dot(left, l_ref[f], preferred_element_type=F32)
        y = y[:count] + (y[count : 2 * count] + y[2 * count :])
        if not spectra:
            lower = jnp.concatenate([y[:, frames:], -y[:, :frames]], axis=1)
            o_ref[f] = jnp.concatenate([y, lower], axis=0).astype(BF16)
            return carry
        for c in range(2):
            for i in range(tiles):
                v = y[:, c * frames + i * LANES : c * frames + (i + 1) * LANES]
                rows[0][i, pl.ds(c * count * pitch + f, count, stride=pitch), :] = v
        return carry

    lax.fori_loop(0, share, one, 0, unroll=8)
    if not spectra:
        return
    for i in range(tiles):
        v = rows[0][i].reshape(2, count, pitch, LANES)[:, :, :share]
        o_ref[:, :, :, i * LANES : (i + 1) * LANES] = v


def apply(table, mixing, stacked, count, spectra):
    shares, share = mixing.shape[:2]
    bins, frames = stacked.shape[0], stacked.shape[2] // 2
    block = pl.BlockSpec((share,) + stacked.shape[1:], lambda r, table: (table[r], 0, 0))
    scratch = [VMEM((share * count, LANES), F32)]
    if spectra:
        shape = jax.ShapeDtypeStruct((2, count, bins, frames), F32)
        out = pl.BlockSpec((2, count, share, frames), lambda r, table: (0, 0, table[r], 0))
        scratch.append(VMEM((frames // LANES, 2 * count * (share + 8), LANES), F32))
    else:
        shape, out = jax.ShapeDtypeStruct(stacked.shape, BF16), block
    return pl.pallas_call(
        functools.partial(apply_kernel, count=count, spectra=spectra),
        grid_spec=pltpu.PrefetchScalarGridSpec(
            num_scalar_prefetch=1,
            grid=(shares,),
            in_specs=[pl.BlockSpec((1,) + mixing.shape[1:], lambda r, table: (r, 0, 0)), block],
            out_specs=out,
            scratch_shapes=scratch,
        ),
        out_shape=shape,
        compiler_params=options(),
        cost_estimate=cost(
            16 * count * count * bins * frames, stacked.size * 2 + 8 * count * bins * frames
        ),
        name="apply" if spectra else "whitened",
    )(table, mixing, stacked)


def on_device(spectra, norm_gain, w_in, b_in, w_mid, b_mid, w_out, b_out):
    _, count, bins, frames = spectra.shape
    owners, devices = lax.axis_size("freq"), lax.axis_size("frame")
    mine, position = lax.axis_index("freq"), lax.axis_index("frame")
    each, chunks, share, depth = GROUP // owners, count // GROUP, bins // devices, devices // 2
    place = jnp.reshape(mine, (1,)).astype(jnp.int32)
    side, level = position & 1, position >> 1
    order = jnp.arange(depth, dtype=jnp.int32)
    keep = (side * depth + (level ^ order)).astype(jnp.int32)
    send = ((side ^ 1) * depth + (level ^ order)).astype(jnp.int32)

    def column(v):
        return jnp.broadcast_to(v[:, None], (v.shape[0], LANES))

    weights = (
        column(norm_gain), w_in.T, column(b_in), w_mid.T, column(b_mid), w_out.T, column(b_out),
    )
    *powers, stacked = prepare(spectra, place, owners, each, chunks)

    def shared(mixing):
        near = [mixing] + [exchange(mixing, "frame", 2 * r) for r in range(1, depth)]
        return jnp.stack(near + [exchange(v, "frame", 1) for v in near])

    every = jnp.concatenate([keep, send])
    factor, inverse, unmixing = whiten(keep, stacked, count, share)
    white = apply(every, shared(unmixing), stacked, count, False)

    arrived = []
    for c in range(chunks):
        pieces = powers[c * owners : (c + 1) * owners]
        arrived.append([pieces[0]] + [exchange(pieces[m], "freq", m) for m in range(1, owners)])
    modelled = []
    for c in range(chunks):
        out = model(arrived[c], place, weights)
        modelled.append([out[0]] + [exchange(out[m], "freq", m) for m in range(1, owners)])

    laid = []
    variances = place
    for c in range(chunks):
        sent, variances = covariance(send, place, white, modelled[c], variances, c, count, BF16)
        kept, variances = covariance(keep, place, white, modelled[c], variances, c, count, F32)
        parts = [None] * depth
        for r in list(range(1, depth)) + [0]:
            v = kept[r] + exchange(sent[r], "frame", 1)
            parts[r] = v if r == 0 else exchange(v.astype(BF16), "frame", 2 * r)
        laid.append(unpack(parts, count, share))

    mixing = sweep(laid, factor, inverse, count, share, frames * devices)
    demixed = apply(every, shared(mixing), stacked, count, True)
    return demixed, variances


def solution(mesh):
    in_specs = (P(None, None, "freq", "frame"), P(), P(), P(), P(), P(), P(), P())
    out_specs = (P(None, None, "freq", "frame"), P(None, "freq", "frame"))
    return jax.shard_map(
        on_device, mesh=mesh, in_specs=in_specs, out_specs=out_specs, check_vma=False
    )
```

```python
import functools

import jax
import jax.numpy as jnp
from jax import lax
from jax.experimental import pallas as pl
from jax.experimental.pallas import tpu as pltpu
from jax.sharding import PartitionSpec as P

epsilon = 1e-05
power_floor = 0.001
variance_floor = 0.25
ridge = 2.0**-14
floor = 1e-8
GROUP = 8
LANES = 128
BF16 = jnp.bfloat16
F32 = jnp.float32
SMEM = pltpu.SMEM
VMEM = pltpu.VMEM


def options(mib=48):
    return pltpu.CompilerParams(vmem_limit_bytes=mib * 1024 * 1024)


def cost(flops, moved, transcendentals=0):
    return pl.CostEstimate(
        flops=int(flops), bytes_accessed=int(moved), transcendentals=int(transcendentals)
    )


def exchange(value, axis, mask):
    size = lax.axis_size(axis)
    return lax.ppermute(value, axis, [(i, i ^ mask) for i in range(size)])


def power_kernel(place, x_ref, *outs, owners, each, chunks):
    mine = place[0]
    for c in range(chunks):
        for m in range(owners):
            for i in range(each):
                source = c * GROUP + (mine ^ m) * each + i
                re = x_ref[0, source].astype(F32)
                im = x_ref[1, source].astype(F32)
                v = jnp.log(re * re + im * im + power_floor).astype(BF16)
                outs[c * (owners // 2) + m // 2][m % 2, i] = v


def power(spectra, place, owners, each, chunks):
    _, count, bins, frames = spectra.shape
    step = 32
    pairs = chunks * owners // 2
    block = pl.BlockSpec((2, each, step, frames), lambda b: (0, 0, b, 0))
    return pl.pallas_call(
        functools.partial(power_kernel, owners=owners, each=each, chunks=chunks),
        grid=(bins // step,),
        in_specs=[
            pl.BlockSpec(memory_space=SMEM),
            pl.BlockSpec((2, count, step, frames), lambda b: (0, 0, b, 0)),
        ],
        out_specs=[block] * pairs,
        out_shape=[jax.ShapeDtypeStruct((2, each, bins, frames), BF16)] * pairs,
        compiler_params=options(),
        cost_estimate=cost(5 * spectra.size, 3 * spectra.size, spectra.size // 2),
        name="power",
    )(place, spectra)


def stack_kernel(x_ref, l_ref, rows, *, count):
    bins, frames = x_ref.shape[2], x_ref.shape[3]
    wide = frames // LANES
    pitch = rows.shape[1] // (2 * count)
    for i in range(wide):
        block = x_ref[:, :, :, i * LANES : (i + 1) * LANES].astype(F32)
        block = block.reshape(2 * count, bins, LANES)
        for n in range(2 * count):
            rows[i, n * pitch : n * pitch + bins] = block[n]

    def one(f, carry):
        both = jnp.concatenate(
            [rows[i, pl.ds(f, 2 * count, stride=pitch), :] for i in range(wide)], axis=1
        )
        re, im = both[:count], both[count:]
        upper = jnp.concatenate([re, im], axis=1)
        lower = jnp.concatenate([im, -re], axis=1)
        l_ref[f] = jnp.concatenate([upper, lower], axis=0).astype(BF16)
        return carry

    lax.fori_loop(0, bins, one, 0, unroll=8)


def stack(spectra):
    _, count, bins, frames = spectra.shape
    step = 16
    return pl.pallas_call(
        functools.partial(stack_kernel, count=count),
        grid=(bins // step,),
        in_specs=[pl.BlockSpec((2, count, step, frames), lambda b: (0, 0, b, 0))],
        out_specs=pl.BlockSpec((step, 2 * count, 2 * frames), lambda b: (b, 0, 0)),
        out_shape=jax.ShapeDtypeStruct((bins, 2 * count, 2 * frames), BF16),
        scratch_shapes=[VMEM((frames // LANES, 2 * count * (step + 8), LANES), F32)],
        compiler_params=options(),
        cost_estimate=cost(5 * spectra.size, 6 * spectra.size),
        name="stack",
    )(spectra)


def turn_kernel(*refs):
    count = len(refs) // 2
    size = refs[0].shape[1]
    row = lax.broadcasted_iota(jnp.int32, (size, size), 0)
    column = lax.broadcasted_iota(jnp.int32, (size, size), 1)
    unit = jnp.where(row == column, 1.0, 0.0).astype(BF16)
    for w, o in zip(refs[:count], refs[count:]):
        v = lax.dot_general(unit, w[...], (((1,), (1,)), ((), ())), preferred_element_type=F32)
        o[...] = v.astype(BF16)


def turn(weights):
    size = 256
    rows, columns = weights[0].shape
    return pl.pallas_call(
        turn_kernel,
        grid=(columns // size,),
        in_specs=[pl.BlockSpec((rows, size), lambda n: (0, n))] * len(weights),
        out_specs=[pl.BlockSpec((size, rows), lambda n: (n, 0))] * len(weights),
        out_shape=[jax.ShapeDtypeStruct((columns, rows), BF16)] * len(weights),
        compiler_params=options(),
        cost_estimate=cost(2 * rows * columns * size * 3, 12 * rows * columns),
        name="turn",
    )(*weights)


def silu(v):
    return v / (1.0 + jnp.exp(-v))


def softplus(v):
    return jnp.maximum(v, 0.0) + jnp.log1p(jnp.exp(-jnp.abs(v)))


def model_kernel(place, *refs, owners):
    pieces = refs[:owners]
    own, others = refs[owners + 7], refs[owners + 8 : owners + 7 + owners // 2]
    outs = [own.at[0], own.at[1]] + [o.at[e] for o in others for e in range(2)]
    gain, w_in, b_in, w_mid, b_mid, w_out, b_out = refs[owners : owners + 7]
    normed, hidden = refs[owners + 7 + owners // 2 :]
    mine = place[0]
    bins, frames = pieces[0].shape[1:]
    total = bins * owners
    wide = frames // LANES

    def spread(column):
        return jnp.concatenate([column] * wide, axis=1)

    values = [piece[0].astype(F32) for piece in pieces]
    average = sum(jnp.sum(v, axis=0, keepdims=True) for v in values) / total
    values = [v - average for v in values]
    square = sum(jnp.sum(v * v, axis=0, keepdims=True) for v in values) / total
    scale = lax.rsqrt(square + epsilon)
    for m in range(owners):
        at = pl.multiple_of((mine ^ m) * bins, bins)
        normed[pl.ds(at, bins), :] = (
            values[m] * scale * spread(gain[pl.ds(at, bins), :])
        ).astype(BF16)

    tile = 256

    def layer(weights, bias, source, target):
        def one(h, carry):
            at = pl.multiple_of(h * tile, tile)
            v = jnp.dot(weights[pl.ds(at, tile), :], source[...], preferred_element_type=F32)
            target[pl.ds(at, tile), :] = silu(v + spread(bias[pl.ds(at, tile), :])).astype(BF16)
            return carry

        lax.fori_loop(0, weights.shape[0] // tile, one, 0, unroll=4)

    layer(w_in, b_in, normed, hidden)
    layer(w_mid, b_mid, hidden, normed)
    for m in range(owners):
        at = pl.multiple_of((mine ^ m) * bins, bins)
        v = jnp.dot(w_out[pl.ds(at, bins), :], normed[...], preferred_element_type=F32)
        outs[m][0] = (softplus(v + spread(b_out[pl.ds(at, bins), :])) + variance_floor).astype(
            BF16
        )


def model(pieces, place, weights):
    owners = len(pieces)
    _, each, bins, frames = pieces[0][0].shape
    hidden = weights[1].shape[0]

    def spec(lead):
        return pl.BlockSpec((None, 1, bins, frames), lambda i: (lead, i, 0, 0))

    whole = [pl.BlockSpec(w.shape, lambda i: (0, 0)) for w in weights]
    return pl.pallas_call(
        functools.partial(model_kernel, owners=owners),
        grid=(each,),
        in_specs=[pl.BlockSpec(memory_space=SMEM)] + [spec(lead) for _, lead in pieces] + whole,
        out_specs=[pl.BlockSpec((2, 1, bins, frames), lambda i: (0, i, 0, 0))] * (owners // 2),
        out_shape=[jax.ShapeDtypeStruct((2, each, bins, frames), BF16)] * (owners // 2),
        scratch_shapes=[VMEM((hidden, frames), BF16), VMEM((hidden, frames), BF16)],
        compiler_params=options(),
        cost_estimate=cost(
            6 * each * hidden * hidden * frames, 6 * hidden * hidden, 8 * each * hidden * frames
        ),
        name="source_model",
    )(place, *[v for v, _ in pieces], *weights)


def spread_over_row(pairs):
    crossed = [exchange(v, "freq", 2 * (i + 1)) for i, v in enumerate(pairs[1:])]
    passed = jnp.stack([pairs[0][1]] + [v[1] for v in crossed])
    passed = exchange(passed, "freq", 1)
    pieces = [(pairs[0], 0), (passed, 0)]
    for i, v in enumerate(crossed):
        pieces += [(v, 0), (passed, i + 1)]
    return pieces


def covariance_kernel(table, place, l_ref, *refs, owners, count):
    pieces, (o_ref, natural, weight) = refs[:owners], refs[-3:]
    mine = place[0]
    each, bins, frames = pieces[0].shape
    for m in range(owners):
        for i in range(each):
            source = (mine ^ m) * each + i
            natural[source] = pieces[m][i]
            weight[source] = 1.0 / pieces[m][i].astype(F32)
    shape = (count, GROUP * count)
    row = lax.broadcasted_iota(jnp.int32, shape, 0)
    column = lax.rem(lax.broadcasted_iota(jnp.int32, shape, 1), count)
    real = row <= column
    quarter = bins // 4
    together = min(4, quarter)

    def weighted(f):
        left = l_ref[f]
        top = left.astype(F32)[:count]
        parts = []
        for j in range(GROUP):
            w = weight[j, pl.ds(f, 1), :]
            parts.append(top * jnp.concatenate([w, w], axis=1))
        return left, jnp.concatenate(parts, axis=0).astype(BF16)

    def summed(left, right):
        dims = (((1,), (1,)), ((), ()))
        v = lax.dot_general(left, right, dims, preferred_element_type=F32)
        return jnp.where(real, v[:count], v[count:])

    def some(n, carry):
        first = n * together
        operands = [weighted(first + i + e * quarter) for i in range(together) for e in range(4)]
        sums = [summed(*o) for o in operands]
        for i in range(together):
            v = sums[4 * i : 4 * i + 4]
            rows = [jnp.concatenate([v[e], v[e + 2]], axis=1) for e in range(2)]
            o_ref[0, first + i] = jnp.concatenate(rows, axis=0).astype(o_ref.dtype)
        return carry

    lax.fori_loop(0, quarter // together, some, 0)


def covariance(table, place, stacked, pieces, natural, chunk, count, held, after):
    owners, shares = len(pieces), table.shape[0]
    _, each, bins, frames = pieces[0][0].shape
    share = stacked.shape[0] // lax.axis_size("frame")

    def piece(lead):
        block = (None, each, share, frames)
        return pl.BlockSpec(block, lambda r, table, place: (lead, 0, table[r], 0))

    lanes = 2 * GROUP * count
    extra = ([] if natural is None else [natural]) + list(after)
    return pl.pallas_call(
        functools.partial(covariance_kernel, owners=owners, count=count),
        grid_spec=pltpu.PrefetchScalarGridSpec(
            num_scalar_prefetch=2,
            grid=(shares,),
            in_specs=[
                pl.BlockSpec(
                    (share,) + stacked.shape[1:], lambda r, table, place: (table[r], 0, 0)
                )
            ]
            + [piece(lead) for _, lead in pieces]
            + [pl.BlockSpec(memory_space=pl.ANY)] * len(extra),
            out_specs=[
                pl.BlockSpec(
                    (1, share // 4, 2 * count, lanes), lambda r, table, place: (r, 0, 0, 0)
                ),
                pl.BlockSpec(
                    (GROUP, share, frames), lambda r, table, place: (chunk, table[r], 0)
                ),
            ],
            scratch_shapes=[VMEM((GROUP, share, frames), F32)],
        ),
        out_shape=[
            jax.ShapeDtypeStruct((shares, share // 4, 2 * count, lanes), held),
            jax.ShapeDtypeStruct((count, bins, frames), BF16),
        ],
        input_output_aliases={} if natural is None else {3 + owners: 1},
        compiler_params=options(),
        cost_estimate=cost(
            shares * share * 24 * count * count * GROUP * frames,
            shares * share * (8 * count * frames + 4 * count * count * GROUP),
        ),
        name="covariance",
    )(table, place, stacked, *[v for v, _ in pieces], *extra)


def unpack_kernel(*refs, count, share, lanes_b):
    parts, o_ref, added, turned = refs[:-3], refs[-3], refs[-2], refs[-1]
    half = GROUP * count
    blocks = o_ref.shape[1]

    v = parts[0][...].astype(F32)
    for part in parts[1:]:
        v = v + part[...].astype(F32)
    added[...] = v

    def turn(a, carry):
        v, w = added[:, a, :], added[:, count + a, :]
        v = jnp.concatenate([v[:, :half], w[:, :half], v[:, half:], w[:, half:]], axis=0)
        turned[a, :, 0:share] = v.T
        return carry

    lax.fori_loop(0, count, turn, 0, unroll=8)

    def lay(a, carry):
        for g in range(blocks):
            re, im = [], []
            for i in range(lanes_b):
                b = g * lanes_b + i
                if b >= count:
                    re.append(jnp.zeros((GROUP, share), F32))
                    im.append(jnp.zeros((GROUP, share), F32))
                    continue
                low, high = jnp.minimum(a, b), jnp.maximum(a, b)
                sign = jnp.where(a > b, 1.0, jnp.where(a < b, -1.0, 0.0))
                re.append(turned[low, pl.ds(high, GROUP, stride=count), :][:, :share])
                im.append(turned[high, pl.ds(low, GROUP, stride=count), :][:, :share] * sign)
            o_ref[a, g, 0] = jnp.concatenate(re, axis=1)
            o_ref[a, g, 1] = jnp.concatenate(im, axis=1)
        return carry

    lax.fori_loop(0, count, lay, 0, unroll=4)


def unpack(parts, count, share):
    lanes_b = LANES // share
    blocks = -(-count // lanes_b)
    shape = (count, blocks, 2, GROUP, LANES)
    return pl.pallas_call(
        functools.partial(unpack_kernel, count=count, share=share, lanes_b=lanes_b),
        out_shape=jax.ShapeDtypeStruct(shape, F32),
        scratch_shapes=[VMEM(parts[0].shape, F32), VMEM((count, GROUP * count, LANES), F32)],
        compiler_params=options(),
        cost_estimate=cost(10 * parts[0].size, 4 * parts[0].size * (len(parts) + 2)),
        name="unpack",
    )(*parts)


def sweep_kernel(*refs, count, share, frames):
    chunks = count // GROUP
    v_refs = refs[:chunks]
    factor, inverse_ref, o_ref, wr, wi, diagonal, flat = refs[chunks:]
    lanes_b = LANES // share
    blocks = v_refs[0].shape[1]
    full = (GROUP, LANES)
    sub = lax.broadcasted_iota(jnp.int32, full, 0)
    lane = lax.broadcasted_iota(jnp.int32, full, 1)
    group = [(lane >= i * share) & (lane < (i + 1) * share) for i in range(lanes_b)]
    zero = jnp.zeros(full, F32)

    wr[...] = jnp.zeros_like(wr)
    wi[...] = jnp.zeros_like(wi)
    for c in range(chunks):
        for g in range(blocks):

            def own(a, carry):
                lr, li = factor[a, 0, c], factor[a, 1, c]
                vr, vi = v_refs[c][a, g, 0], v_refs[c][a, g, 1]
                return carry[0] + lr * vr - li * vi, carry[1] + lr * vi + li * vr

            first = lax.fori_loop(0, (c + 1) * GROUP, own, (zero, zero), unroll=4)
            diagonal[c, g, 0], diagonal[c, g, 1] = first

    def total(x):
        shift = share
        while shift < LANES:
            x = x + pltpu.roll(x, shift, 1)
            shift *= 2
        return x

    for k in range(count):
        ck, sk = divmod(k, GROUP)
        used = k // lanes_b + 1
        for a in range(k + 1):
            wr[a, ck] = wr[a, ck] + jnp.where(sub == sk, factor[a, 0, ck], 0.0)
            wi[a, ck] = wi[a, ck] + jnp.where(sub == sk, factor[a, 1, ck], 0.0)
        pick_r, pick_i = [], []
        for g in range(used):
            pr, pi = zero, zero
            for i in range(lanes_b):
                b = g * lanes_b + i
                if b <= k:
                    pr = jnp.where(group[i], wr[b, ck, sk : sk + 1, :], pr)
                    pi = jnp.where(group[i], wi[b, ck, sk : sk + 1, :], pi)
            pick_r.append(pr)
            pick_i.append(pi)

        def product(load):
            ur, ui = zero, zero
            for g in range(used):
                vr, vi = load(g, 0), load(g, 1)
                ur = ur + vr * pick_r[g] + vi * pick_i[g]
                ui = ui + vi * pick_r[g] - vr * pick_i[g]
            return ur, ui

        def gather(a, carry):
            out = []
            kr = wr[a, ck, sk : sk + 1, :]
            ki = wi[a, ck, sk : sk + 1, :]
            for c in range(chunks):
                nr, ni, de = carry[3 * c : 3 * c + 3]
                ur, ui = product(lambda g, part: v_refs[c][a, g, part])
                ar, ai = wr[a, c], wi[a, c]
                out.append(nr + ar * ur - ai * ui)
                out.append(ni + ar * ui + ai * ur)
                out.append(de + kr * ur - ki * ui)
            return tuple(out)

        sums = lax.fori_loop(0, k + 1, gather, (zero,) * (3 * chunks), unroll=min(2, k + 1))
        steer = []
        for c in range(chunks):
            nr, ni, de = sums[3 * c : 3 * c + 3]
            if (c + 1) * GROUP > k + 1:
                ur, ui = product(lambda g, part: diagonal[c, g, part])
                later = sub + c * GROUP > k
                nr = nr + jnp.where(later, ur, 0.0)
                ni = ni + jnp.where(later, ui, 0.0)
            nr, ni, de = total(nr), total(ni), total(de)
            inverse = 1.0 / de
            vr, vi = nr * inverse, ni * inverse
            if c == ck:
                vr = jnp.where(sub == sk, 1.0 - lax.rsqrt(de / frames), vr)
                vi = jnp.where(sub == sk, 0.0, vi)
            steer.append((vr, vi))

        def update(a, carry):
            kr = jnp.broadcast_to(wr[a, ck, sk : sk + 1, :], full)
            ki = jnp.broadcast_to(wi[a, ck, sk : sk + 1, :], full)
            for c in range(chunks):
                vr, vi = steer[c]
                wr[a, c] = wr[a, c] - (vr * kr - vi * ki)
                wi[a, c] = wi[a, c] - (vr * ki + vi * kr)
            return carry

        lax.fori_loop(0, k + 1, update, 0, unroll=min(2, k + 1))

    for a in range(count):

        def product(b, carry):
            tr = inverse_ref[a, 0, pl.ds(b, 1), :]
            ti = inverse_ref[a, 1, pl.ds(b, 1), :]
            out = []
            for c in range(chunks):
                r, i = wr[b, c], wi[b, c]
                out.append(carry[2 * c] + r * tr - i * ti)
                out.append(carry[2 * c + 1] + r * ti + i * tr)
            return tuple(out)

        sums = lax.fori_loop(a, count, product, (zero,) * (2 * chunks), unroll=min(4, count - a))
        for c in range(chunks):
            at = c * GROUP * 2 * count + a
            flat[pl.ds(at, GROUP, stride=2 * count), :] = sums[2 * c]
            flat[pl.ds(at + count, GROUP, stride=2 * count), :] = -sums[2 * c + 1]
    flatten(flat, o_ref, share)


def flatten(flat, o_ref, share):
    for i in range(flat.shape[0] // LANES):
        v = flat[i * LANES : (i + 1) * LANES, :].T[:share]
        o_ref[:, i * LANES : (i + 1) * LANES] = v.astype(o_ref.dtype)


def whiten_kernel(table, l_ref, inverse_ref, o_ref, raw, ar, ai, flat, *, count, frames):
    share = l_ref.shape[0]
    chunks = count // GROUP
    wide = 2 * count
    copies = LANES // share
    dims = (((1,), (1,)), ((), ()))

    def sums(f, carry):
        left = l_ref[f]
        v = lax.dot_general(left, left, dims, preferred_element_type=F32)
        at = pl.multiple_of(f * wide, wide)
        pad = jnp.zeros((wide, LANES - wide), F32)
        raw[pl.ds(at, wide), :] = jnp.concatenate([v * (1.0 / frames), pad], axis=1)
        return carry

    lax.fori_loop(0, share, sums, 0, unroll=8)

    def turn(a, carry):
        re = raw[pl.ds(a, share, stride=wide), :].T[:count]
        im = raw[pl.ds(count + a, share, stride=wide), :].T[:count]
        ar[a] = jnp.concatenate([re] * copies, axis=1)
        ai[a] = jnp.concatenate([-im] * copies, axis=1)
        return carry

    lax.fori_loop(0, count, turn, 0, unroll=4)
    row = lax.broadcasted_iota(jnp.int32, (count, LANES), 0)
    zero = jnp.zeros((count, LANES), F32)

    def begin(a, carry):
        inverse_ref[a, 0] = jnp.where(row == a, 1.0, 0.0)
        inverse_ref[a, 1] = zero
        ar[a] = ar[a] + jnp.where(row == a, ar[a] * ridge + floor, 0.0)
        return carry

    lax.fori_loop(0, count, begin, 0, unroll=4)
    for k in range(count):
        scale = lax.rsqrt(ar[k, k : k + 1, :])
        lr = jnp.where(row >= k, ar[k] * scale, 0.0)
        li = jnp.where(row > k, ai[k] * scale, 0.0)
        ar[k], ai[k] = lr, li

        def right(b, carry):
            br, bi = ar[k, pl.ds(b, 1), :], ai[k, pl.ds(b, 1), :]
            ar[b] = ar[b] - (lr * br + li * bi)
            ai[b] = ai[b] - (li * br - lr * bi)
            return carry

        if k + 1 < count:
            lax.fori_loop(k + 1, count, right, 0, unroll=min(2, count - k - 1))

        def left(b, carry):
            tr = inverse_ref[b, 0, k : k + 1, :] * scale
            ti = inverse_ref[b, 1, k : k + 1, :] * scale
            r, i = inverse_ref[b, 0], inverse_ref[b, 1]
            nr, ni = r - (lr * tr - li * ti), i - (lr * ti + li * tr)
            inverse_ref[b, 0] = jnp.where(row == k, tr, nr)
            inverse_ref[b, 1] = jnp.where(row == k, ti, ni)
            return carry

        lax.fori_loop(0, k + 1, left, 0, unroll=min(2, k + 1))
    for a in range(count):
        for part in range(2):
            inverse_ref[a, part] = inverse_ref[a, part].astype(BF16).astype(F32)
        for c in range(chunks):
            at = c * GROUP * wide + a
            rows = slice(c * GROUP, (c + 1) * GROUP)
            flat[pl.ds(at, GROUP, stride=wide), :] = inverse_ref[a, 0, rows, :]
            flat[pl.ds(at + count, GROUP, stride=wide), :] = -inverse_ref[a, 1, rows, :]
    flatten(flat, o_ref, share)


def whiten(table, stacked, count, share):
    wide, frames = 2 * count, stacked.shape[2] // 2
    shapes = [(count, 2, count, LANES), (share, wide * count)]
    state = VMEM((count, count, LANES), F32)
    return pl.pallas_call(
        functools.partial(whiten_kernel, count=count, frames=frames),
        grid_spec=pltpu.PrefetchScalarGridSpec(
            num_scalar_prefetch=1,
            grid=(1,),
            in_specs=[
                pl.BlockSpec((share,) + stacked.shape[1:], lambda r, table: (table[0], 0, 0))
            ],
            out_specs=[
                pl.BlockSpec(x, functools.partial(lambda n, r, table: (0,) * n, len(x)))
                for x in shapes
            ],
            scratch_shapes=[
                VMEM((share * wide, LANES), F32), state, state, VMEM((wide * count, LANES), F32),
            ],
        ),
        out_shape=[jax.ShapeDtypeStruct(x, t) for x, t in zip(shapes, (F32, BF16))],
        compiler_params=options(),
        cost_estimate=cost(3000 * count**3, share * stacked.shape[1] * stacked.shape[2] * 2),
        name="whiten",
    )(table, stacked)


def sweep(parts, factor, inverse, count, share, frames):
    chunks = count // GROUP
    blocks = parts[0].shape[1]
    state = VMEM((count, chunks, GROUP, LANES), F32)
    return pl.pallas_call(
        functools.partial(sweep_kernel, count=count, share=share, frames=frames),
        out_shape=jax.ShapeDtypeStruct((share, 2 * count * count), F32),
        scratch_shapes=[
            state,
            state,
            VMEM((chunks, blocks, 2, GROUP, LANES), F32),
            VMEM((2 * count * count, LANES), F32),
        ],
        compiler_params=options(),
        cost_estimate=cost(4500 * count**3, 4 * 3 * parts[0].size),
        name="sweep",
    )(*parts, factor, inverse)


def invert_kernel(t_ref, factor, lr, li, *, count):
    row = lax.broadcasted_iota(jnp.int32, (count, LANES), 0)
    for a in range(count):
        lr[a] = jnp.where(row == a, 1.0, 0.0)
        li[a] = jnp.zeros((count, LANES), F32)
    for k in range(count):
        scale = 1.0 / t_ref[k, 0, k : k + 1, :]
        tr = jnp.where(row > k, t_ref[k, 0], 0.0)
        ti = jnp.where(row > k, t_ref[k, 1], 0.0)

        def left(b, carry):
            r, i = lr[b], li[b]
            kr, ki = lr[b, k : k + 1, :] * scale, li[b, k : k + 1, :] * scale
            lr[b] = jnp.where(row == k, kr, r - (tr * kr - ti * ki))
            li[b] = jnp.where(row == k, ki, i - (tr * ki + ti * kr))
            return carry

        lax.fori_loop(0, k + 1, left, 0, unroll=min(2, k + 1))
    for a in range(count):
        for c in range(count // GROUP):
            factor[a, 0, c] = lr[a, c * GROUP : (c + 1) * GROUP, :]
            factor[a, 1, c] = li[a, c * GROUP : (c + 1) * GROUP, :]


def invert(t, count):
    state = VMEM((count, count, LANES), F32)
    shape = (count, 2, count // GROUP, GROUP, LANES)
    return pl.pallas_call(
        functools.partial(invert_kernel, count=count),
        out_shape=jax.ShapeDtypeStruct(shape, F32),
        scratch_shapes=[state, state],
        compiler_params=options(),
        cost_estimate=cost(1500 * count**3, 8 * t.size),
        name="invert",
    )(t)


def apply_kernel(table, l_ref, *refs, sources, count, spectra):
    w_refs = refs[: len(sources)]
    o_ref, mixing, *rows = refs[len(refs) - (3 if spectra else 2) :]
    share = l_ref.shape[0]
    frames = l_ref.shape[2] // 2
    wide = 2 * count
    tiles = frames // LANES
    pitch = share + 8
    pad = jnp.zeros((share, LANES - wide), F32)
    step = 0
    for ref, size in zip(w_refs, sources):
        for n in range(size):

            @pl.when(pl.program_id(0) == step)
            def load(ref=ref, n=n):
                for j in range(count):
                    v = ref[n, :, j * wide : (j + 1) * wide].astype(F32)
                    v = jnp.concatenate([v, pad], axis=1)
                    mixing[pl.ds(j, share, stride=count), :] = v

            step += 1

    def one(f, carry):
        at = pl.multiple_of(f * count, count)
        w = mixing[pl.ds(at, count), 0:wide]
        if not spectra:
            y = jnp.dot(w.astype(BF16), l_ref[f], preferred_element_type=F32)
            lower = jnp.concatenate([y[:, frames:], -y[:, :frames]], axis=1)
            o_ref[f] = jnp.concatenate([y, lower], axis=0).astype(BF16)
            return carry
        high = w.astype(BF16).astype(F32)
        middle = (w - high).astype(BF16).astype(F32)
        low = w - high - middle
        left = jnp.concatenate([high, middle, low], axis=0).astype(BF16)
        y = jnp.dot(left, l_ref[f], preferred_element_type=F32)
        y = y[:count] + (y[count : 2 * count] + y[2 * count :])
        for c in range(2):
            for i in range(tiles):
                v = y[:, c * frames + i * LANES : c * frames + (i + 1) * LANES]
                rows[0][i, pl.ds(c * count * pitch + f, count, stride=pitch), :] = v
        return carry

    lax.fori_loop(0, share, one, 0, unroll=8)
    if not spectra:
        return
    for i in range(tiles):
        v = rows[0][i].reshape(2, count, pitch, LANES)[:, :, :share]
        o_ref[:, :, :, i * LANES : (i + 1) * LANES] = v


def apply(table, mixings, stacked, into, count, spectra):
    shares, share = table.shape[0], mixings[0].shape[1]
    bins, frames = stacked.shape[0], stacked.shape[2] // 2
    block = pl.BlockSpec((share,) + stacked.shape[1:], lambda r, table: (table[r], 0, 0))
    scratch = [VMEM((share * count, LANES), F32)]
    if spectra:
        shape = jax.ShapeDtypeStruct((2, count, bins, frames), F32)
        out = pl.BlockSpec((2, count, share, frames), lambda r, table: (0, 0, table[r], 0))
        scratch.append(VMEM((frames // LANES, 2 * count * (share + 8), LANES), F32))
    else:
        shape, out = jax.ShapeDtypeStruct(stacked.shape, BF16), block
    extra = [] if into is None else [into]
    sources = tuple(m.shape[0] for m in mixings)
    return pl.pallas_call(
        functools.partial(apply_kernel, sources=sources, count=count, spectra=spectra),
        grid_spec=pltpu.PrefetchScalarGridSpec(
            num_scalar_prefetch=1,
            grid=(shares,),
            in_specs=[block]
            + [pl.BlockSpec(m.shape, lambda r, table: (0, 0, 0)) for m in mixings]
            + [pl.BlockSpec(memory_space=pl.ANY)] * len(extra),
            out_specs=out,
            scratch_shapes=scratch,
        ),
        out_shape=shape,
        input_output_aliases={2 + len(mixings): 0} if extra else {},
        compiler_params=options(),
        cost_estimate=cost(
            16 * count * count * shares * share * frames,
            (12 if spectra else 8) * count * shares * share * frames,
        ),
        name="apply" if spectra else "whitened",
    )(table, stacked, *mixings, *extra)


def on_device(spectra, norm_gain, w_in, b_in, w_mid, b_mid, w_out, b_out):
    _, count, bins, frames = spectra.shape
    owners, devices = lax.axis_size("freq"), lax.axis_size("frame")
    mine, position = lax.axis_index("freq"), lax.axis_index("frame")
    each, chunks, share, depth = GROUP // owners, count // GROUP, bins // devices, devices // 2
    place = jnp.reshape(mine, (1,)).astype(jnp.int32)
    side, level = position & 1, position >> 1

    def shares(other, masks):
        masks = jnp.asarray(masks, jnp.int32)
        return ((side ^ other) * depth + (level ^ masks)).astype(jnp.int32)

    def column(v):
        return jnp.broadcast_to(v[:, None], (v.shape[0], LANES))

    w_in, w_mid, w_out = turn([w_in, w_mid, w_out])
    weights = (
        column(norm_gain), w_in, column(b_in), w_mid, column(b_mid), w_out, column(b_out),
    )
    pairs = owners // 2
    powers = power(spectra, place, owners, each, chunks)
    arrived = [spread_over_row(powers[c * pairs : (c + 1) * pairs]) for c in range(chunks)]

    stacked = stack(spectra)
    inverse, unmixing = whiten(shares(0, [0]), stacked, count, share)
    factor = invert(inverse, count)
    near, masks, bit = unmixing[None], [0], depth // 2
    while bit:
        near = jnp.concatenate([near, exchange(near, "frame", 2 * bit)])
        masks = masks + [m ^ bit for m in masks]
        bit //= 2
    far = exchange(near, "frame", 1)
    white = apply(shares(0, masks), [near], stacked, None, count, False)
    white = apply(shares(1, masks), [far], stacked, white, count, False)

    modelled = [spread_over_row(model(arrived[c], place, weights)) for c in range(chunks)]

    halves = [list(range(depth // 2, depth)), list(range(depth // 2))]
    laid, variances, done = [], None, []
    for c in range(chunks):
        sent = []
        for h, half in enumerate(halves):
            after = done[-2:-1] if h == 0 else []
            if h == 0 and c == 1:
                after = after + [modelled[chunks - 1][1][0]]
            if h == 0 and c >= 2:
                after = after + [laid[c - 2]]
            v, variances = covariance(
                shares(1, half), place, white, modelled[c], variances, c, count, BF16, after
            )
            sent.append(exchange(v, "frame", 1))
        parts = [None] * depth
        ready = []
        for h, half in enumerate(halves):
            after = done[-1:] if h == 0 else []
            v, variances = covariance(
                shares(0, half), place, white, modelled[c], variances, c, count, F32, after
            )
            for n, r in enumerate(half):
                total = v[n] + sent[h][n]
                parts[r] = total if r == 0 else total.astype(BF16)
            ready.append(parts[half[0]] if h == 0 else parts[half[-1]])
        done += ready
        parts = [parts[0]] + [exchange(parts[r], "frame", 2 * r) for r in range(1, depth)]
        laid.append(unpack(parts, count, share))

    mixing = sweep(laid, factor, inverse, count, share, frames * devices)[None]
    near = [mixing] + [exchange(mixing, "frame", 2 * r) for r in range(1, depth)]
    far = [exchange(v, "frame", 1) for v in near]
    order = list(range(depth))
    demixed = apply(shares(0, order), near, stacked, None, count, True)
    demixed = apply(shares(1, order), far, stacked, demixed, count, True)
    return demixed, variances


def solution(mesh):
    in_specs = (P(None, None, "freq", "frame"), P(), P(), P(), P(), P(), P(), P())
    out_specs = (P(None, None, "freq", "frame"), P(None, "freq", "frame"))
    return jax.shard_map(
        on_device, mesh=mesh, in_specs=in_specs, out_specs=out_specs, check_vma=False
    )
```
